256 devices in a mesh: dom: 128 (over y, z, x), sub: 2 (over core).
Axes of the slice: x: 4, y: 4, z: 8, core: 2. Of those that a mesh axis runs over, the one named last changes fastest.
Arguments:
- rhs: float32 [64, 8, 32768], P(None, None, ('dom', 'sub')), may hold values from -4.5 to 4.5
- inner_tiles: bfloat16 [4, 64, 64, 32768], P(None, None, None, ('dom', 'sub')), may hold values from -0.2 to 1.2, as said below
- inner_cols: int32 [4, 32768], P(None, ('dom', 'sub')), may hold values from 0 to 127, as said below
- send_blocks: int32 [16384], P(('dom', 'sub')), may hold values from 0 to 127
- face_rows: int32 [16384], P(('dom', 'sub')), may hold values from 0 to 127
- face_counts: int32 [256, 2], P(('dom', 'sub')), may hold values from 0 to 32, as said below
- face_tiles: bfloat16 [64, 64, 16384], P(None, None, ('dom', 'sub')), may hold values from -0.1796875 to 0.1796875
- contact_send: int32 [16384], P(('dom', 'sub')), may hold values from 0 to 127
- contact_rows: int32 [16384], P(('dom', 'sub')), may hold values from 0 to 127
- contact_pair: int32 [256, 64], P(('dom', 'sub')), may hold values from 0 to 63, each once within a row
- contact_tiles: bfloat16 [64, 64, 16384], P(None, None, ('dom', 'sub')), may hold values from -0.1796875 to 0.1796875
Outputs:
- adjoint: float32 [64, 8, 32768], P(None, None, ('dom', 'sub'))
- residual: float32 [64, 8, 32768], P(None, None, ('dom', 'sub'))
- normal_residual: float32 [64, 8, 32768], P(None, None, ('dom', 'sub'))
The draws below stay inside these ranges and needn't reach their ends.
Inputs may be any that keep to these rules, and one draw needn't show every extreme that they name: `inner_tiles`: the diagonal tile of each row is the identity plus small entries. `inner_cols`: row 0 names the row's own block. `face_counts`: 0 toward a piece that does not exist; 32 is reached on some piece.
All inputs are finite; a program needn't handle non-finite values.
Results may differ from the reference program's by a relative error of at most 0.003.
Values may be sent and summed in bfloat16 or wider, within the bound.
A program may use at most 128 MiB of HBM per device.

```python
import jax
import jax.numpy as jnp
from jax import lax

BS = 64
NRHS = 8
R = 128
K = 4
S = 32
M = 64
ITERS = 2
NB = 32768
N_DOM = 128
N_SUB = 2
DEVICES = 256


def draw_rhs(key, part):
    key = jax.random.fold_in(key, 11)
    ramp = 0.5 + jnp.arange(NB, dtype=jnp.float32) / NB
    base = jnp.clip(jax.random.normal(key, (BS, NRHS, NB), jnp.float32), -3.0, 3.0)
    return base * ramp[None, None, :]


def draw_inner_tiles(key, part):
    key = jax.random.fold_in(key, 12)
    noise = jnp.clip(0.03 * jax.random.normal(key, (K, BS, BS, NB), jnp.float32), -0.2, 0.2)
    eye = (jnp.arange(BS)[:, None] == jnp.arange(BS)[None, :]).astype(jnp.float32)
    first = (jnp.arange(K) == 0).astype(jnp.float32)
    return (noise + first[:, None, None, None] * eye[None, :, :, None]).astype(jnp.bfloat16)


def draw_inner_cols(key, part):
    key = jax.random.fold_in(key, 13)
    picks = jax.random.randint(key, (K, NB), 0, R, jnp.int32)
    own = jnp.arange(NB, dtype=jnp.int32) % R
    return picks.at[0].set(own)


def draw_face_counts(key, part):
    key = jax.random.fold_in(key, 14)
    counts = jax.random.randint(key, (DEVICES, 2), max(1, S // 4), S + 1, jnp.int32)
    counts = counts.at[DEVICES // 2, 0].set(S)
    counts = counts.at[0, 0].set(0)
    counts = counts.at[DEVICES - 1, 1].set(0)
    return counts


def with_ends(entries, key, least, high):
    longest = entries.shape.index(max(entries.shape))
    spots = []
    for shift in (0, 1):
        where = [jax.random.randint(jax.random.fold_in(key, axis), (), 0, length) for axis, length in enumerate(entries.shape)]
        where[longest] = (where[longest] + shift) % entries.shape[longest]
        spots.append(tuple(where))
    return entries.at[spots[0]].set(least).at[spots[1]].set(high)


def levels(key, shape, cuts, smallest, top_value):
    def one(dim, shards_of):
        draws = jax.random.uniform(jax.random.fold_in(jax.random.fold_in(key, 6), dim), (shards_of,), jnp.float32, smallest / len(cuts), top_value / len(cuts))
        return jnp.repeat(jnp.exp(draws), shape[dim] // shards_of).reshape((-1,) + (1,) * (len(shape) - dim - 1))

    factor_of = one(*cuts[0])
    for cut in cuts[1:]:
        factor_of = factor_of * one(*cut)
    return factor_of


def normal_values(stream_key, shape, scale, most, shards=(), held_as=jnp.bfloat16):
    gain = levels(stream_key, shape, shards, -0.22, 0.18) if shards else 1.0
    array = jax.random.normal(stream_key, shape, jnp.float32) * scale * gain
    return jnp.minimum(jnp.maximum(array, -most), most).astype(held_as)


def setup_inputs(seed: int = 0) -> dict:
    arg_keys = jax.random.split(jax.random.key(seed), 12)
    rhs = draw_rhs(jax.random.fold_in(arg_keys[11], 71), 0)
    inner_tiles = draw_inner_tiles(jax.random.fold_in(arg_keys[11], 71), 0)
    inner_cols = draw_inner_cols(jax.random.fold_in(arg_keys[11], 71), 0)
    send_blocks = with_ends(jax.random.randint(arg_keys[3], (2 * S * DEVICES,), 0, R), jax.random.fold_in(arg_keys[3], 1), 0, R - 1).astype(jnp.int32)
    face_rows = with_ends(jax.random.randint(arg_keys[4], (2 * S * DEVICES,), 0, R), jax.random.fold_in(arg_keys[4], 1), 0, R - 1).astype(jnp.int32)
    face_counts = draw_face_counts(jax.random.fold_in(arg_keys[11], 71), 0)
    face_tiles = normal_values(arg_keys[6], (BS, BS, 2 * S * DEVICES), 0.03, 0.1796875, ((2, 256),))
    contact_send = with_ends(jax.random.randint(arg_keys[7], (M * DEVICES,), 0, R), jax.random.fold_in(arg_keys[7], 1), 0, R - 1).astype(jnp.int32)
    contact_rows = with_ends(jax.random.randint(arg_keys[8], (M * DEVICES,), 0, R), jax.random.fold_in(arg_keys[8], 1), 0, R - 1).astype(jnp.int32)
    contact_pair = jax.vmap(lambda own: jax.random.permutation(own, M))(jax.random.split(arg_keys[9], DEVICES)).reshape((DEVICES, M)).astype(jnp.int32)
    contact_tiles = normal_values(arg_keys[10], (BS, BS, M * DEVICES), 0.03, 0.1796875, ((2, 256),))
    return {"rhs": rhs, "inner_tiles": inner_tiles, "inner_cols": inner_cols, "send_blocks": send_blocks, "face_rows": face_rows, "face_counts": face_counts, "face_tiles": face_tiles, "contact_send": contact_send, "contact_rows": contact_rows, "contact_pair": contact_pair, "contact_tiles": contact_tiles}


def tile_apply(form, tiles, vectors):
    return jnp.einsum(form, tiles.astype(jnp.float32), vectors, precision=lax.Precision.HIGHEST)

def forward(field, inner_tiles, inner_cols, send_blocks, face_rows, face_counts, face_tiles, contact_send, contact_rows, contact_pair, contact_tiles):
    pieces = N_DOM * N_SUB
    blocks = field.shape[2]
    base = jnp.arange(blocks, dtype=jnp.int32) // R * R
    result = jnp.zeros_like(field)
    for index in range(K):
        gathered = jnp.take(field, base + inner_cols[index], axis=2)
        result = result + tile_apply('abj,bnj->anj', inner_tiles[index], gathered)
    slot_ids = jnp.arange(2 * S * pieces, dtype=jnp.int32)
    owner = slot_ids // (2 * S)
    within = slot_ids % (2 * S)
    side = within // S
    place = within % S
    source = owner - 1 + 2 * side
    limit = jnp.where(side == 0, face_counts[owner, 0], face_counts[owner, 1])
    live = ((place < limit) & (source >= 0) & (source < pieces)).astype(jnp.float32)
    source_safe = jnp.clip(source, 0, pieces - 1)
    source_slot = source_safe * (2 * S) + (1 - side) * S + place
    source_block = source_safe * R + send_blocks[source_slot]
    face_terms = tile_apply('abq,bnq->anq', face_tiles, jnp.take(field, source_block, axis=2)) * live
    result = result.at[:, :, owner * R + face_rows].add(face_terms)
    contact_ids = jnp.arange(M * pieces, dtype=jnp.int32)
    holder = contact_ids // M
    partner = jnp.bitwise_xor(holder, pieces // 2)
    partner_block = partner * R + contact_send[partner * M + contact_pair.reshape(-1)]
    contact_terms = tile_apply('abm,bnm->anm', contact_tiles, jnp.take(field, partner_block, axis=2))
    result = result.at[:, :, holder * R + contact_rows].add(contact_terms)
    return result

def reference(rhs, inner_tiles, inner_cols, send_blocks, face_rows, face_counts, face_tiles, contact_send, contact_rows, contact_pair, contact_tiles):

    def apply_forward(field):
        return forward(field, inner_tiles, inner_cols, send_blocks, face_rows, face_counts, face_tiles, contact_send, contact_rows, contact_pair, contact_tiles)

    def apply_adjoint(field):
        unused, pullback = jax.vjp(apply_forward, field)
        return pullback(field)[0]
    adjoint = jnp.zeros_like(rhs)
    residual = rhs
    normal_residual = apply_adjoint(residual)
    direction = normal_residual
    norm_now = lax.optimization_barrier(jnp.sum(normal_residual * normal_residual, axis=(0, 2)))
    for step in range(ITERS):
        image = apply_forward(direction)
        curvature = lax.optimization_barrier(jnp.sum(image * image, axis=(0, 2)))
        alpha = (norm_now / curvature)[None, :, None]
        adjoint = adjoint + alpha * direction
        residual = residual - alpha * image
        normal_residual = apply_adjoint(residual)
        if step + 1 < ITERS:
            norm_next = lax.optimization_barrier(jnp.sum(normal_residual * normal_residual, axis=(0, 2)))
            direction = normal_residual + (norm_next / norm_now)[None, :, None] * direction
            norm_now = norm_next
    return (adjoint, residual, normal_residual)
```

```python
import functools

import jax
import jax.numpy as jnp
from jax import lax
from jax.experimental import pallas as pl
from jax.experimental.pallas import tpu as pltpu
from jax.sharding import PartitionSpec as P

F32 = jnp.float32
BF16 = jnp.bfloat16
APPS = 5
MESH = pl.DeviceIdType.MESH
NT = (((1,), (1,)), ((), ()))


def stage_sizes(devices):
    bits = devices.bit_length() - 1
    first = min(3, bits - 2)
    second = min(3, bits - first - 1)
    return (1 << first, 1 << second, 1 << (bits - first - second))


def low_half(shape):
    return lax.broadcasted_iota(jnp.int32, shape, 1) < 64


def swap(x):
    return pltpu.roll(x, 64, 1)


def pair(x, y):
    low = low_half(x.shape)
    return jnp.where(low, x, swap(y)), jnp.where(low, swap(x), y)


def split(x):
    high = x.astype(BF16)
    return high, (x - high.astype(F32)).astype(BF16)


def split_wide(x):
    high = x.astype(BF16).astype(F32)
    return high, x - high


def dot(a, b):
    return jnp.dot(a, b, preferred_element_type=F32)


def dot_nt(a, b):
    return lax.dot_general(a, b, NT, preferred_element_type=F32)


def split_dot(product, a, b):
    rows = a.shape[0]
    out = product(jnp.concatenate(split(a), axis=0), b)
    return out[:rows] + out[rows:]


def block8(ref, index):
    return ref[pl.ds(pl.multiple_of(index * 8, 8), 8), :]


def put8(ref, index, value):
    ref[pl.ds(pl.multiple_of(index * 8, 8), 8), :] = value


def every8(first, count):
    return pl.ds(first, count, stride=8)


def kernel(
    devices,
    cols_s,
    frows_s,
    crows_s,
    counts_s,
    rhs,
    tiles,
    cols_v,
    send_v,
    rows_v,
    pair_v,
    ftiles,
    ctiles,
    adjoint,
    residual,
    normal,
    wf0,
    wf1,
    w,
    ef,
    e,
    ohk,
    ohs,
    ohst,
    ohr,
    p01,
    p23,
    z0,
    q,
    t,
    f0,
    fw,
    fs,
    u,
    xf,
    ps,
    uo,
    sbuf,
    rbuf,
    arsend,
    arrecv,
    xsend,
    xrecv,
    asend,
    arecv,
):
    me = lax.axis_index("dom") * 2 + lax.axis_index("sub")
    sizes = stage_sizes(devices)

    def place(index):
        return (index // 2, lax.rem(index, 2))

    lower = lax.rem(me + devices - 1, devices)
    upper = lax.rem(me + 1, devices)
    partner = lax.rem(me + devices // 2, devices)

    def group_peers(stage):
        stride = 1
        for size in sizes[:stage]:
            stride *= size
        size = sizes[stage]
        mine = lax.rem(me // stride, size)
        return [me + (lax.rem(mine + i, size) - mine) * stride for i in range(1, size)]

    peers = [group_peers(stage) for stage in range(3)]
    everyone = [lower, upper, partner] + peers[0] + peers[1] + peers[2]

    barrier = pltpu.get_barrier_semaphore()
    for other in everyone:
        pl.semaphore_signal(barrier, inc=1, device_id=place(other), device_id_type=MESH)

    row_id = lax.broadcasted_iota(jnp.int32, (128, 128), 0)
    lane_id = lax.broadcasted_iota(jnp.int32, (128, 128), 1)
    for k in range(4):
        ohk[:, k * 128 : (k + 1) * 128] = jnp.where(
            cols_v[k : k + 1, :] == row_id, 1.0, 0.0
        ).astype(BF16)
    picks = jnp.where(send_v[...] == row_id, 1.0, 0.0)
    ohs[...] = picks.astype(BF16)
    ohst[...] = picks.T.astype(BF16)
    ohr[...] = jnp.where(rows_v[...] == row_id, 1.0, 0.0).astype(BF16)
    eye = jnp.where(row_id == lane_id, 1.0, 0.0).astype(BF16)

    def prepare(a, carry):
        for half, out in ((0, wf0), (1, wf1)):
            x = tiles[2 * half : 2 * half + 2, a].reshape(128, 128)
            x = dot_nt(eye, x)
            out[pl.ds(a, 64, stride=128), :] = x[:64]
            out[pl.ds(64 + a, 64, stride=128), :] = x[64:]
        return carry

    lax.fori_loop(0, 64, prepare, 0, unroll=2)

    def pack(i, carry):
        at = pl.ds(pl.multiple_of(i * 128, 128), 128)
        w[at, 0:128] = wf0[at, :].astype(BF16)
        w[at, 128:256] = wf1[at, :].astype(BF16)
        return carry

    lax.fori_loop(0, 64, pack, 0, unroll=2)

    slot = lax.broadcasted_iota(jnp.int32, (64, 64), 0)
    other_slot = lax.broadcasted_iota(jnp.int32, (64, 64), 1)
    side_a = (slot < 32) & (slot < counts_s[0, 0])
    side_b = (slot >= 32) & (slot - 32 < counts_s[0, 1])
    face_pick = jnp.where((slot == other_slot) & (side_a | side_b), 1.0, 0.0)
    contact_pick = jnp.where(pair_v[...] == slot, 1.0, 0.0)
    slot_pick = jnp.concatenate([face_pick, contact_pick], axis=0).astype(BF16)

    def prepare_slots(a, carry):
        x = jnp.concatenate([ftiles[a], ctiles[a]], axis=0)
        x = dot_nt(slot_pick, x)
        x = jnp.where(low_half((64, 128)), x[:64], x[64:])
        ef[pl.ds(a, 32, stride=128), :] = x[:32]
        ef[pl.ds(64 + a, 32, stride=128), :] = x[32:]
        return carry

    lax.fori_loop(0, 64, prepare_slots, 0, unroll=2)

    def pack_slots(i, carry):
        at = pl.ds(pl.multiple_of(i * 128, 128), 128)
        e[at, :] = ef[at, :].astype(BF16)
        return carry

    lax.fori_loop(0, 32, pack_slots, 0, unroll=2)

    def tile_at(ref, index):
        return ref[pl.ds(pl.multiple_of(index * 128, 128), 128), :]

    low8 = low_half((8, 128))
    zero8 = jnp.zeros((8, 128), F32)

    def spread(field):
        x = field[...]
        y = swap(x)
        low = low_half(x.shape)
        u[0:64] = jnp.where(low, x, y).reshape(64, 8, 128)
        u[64:128] = jnp.where(low, y, x).reshape(64, 8, 128)

    for n in range(8):
        x = rhs[every8(n, 64), :]
        x = jnp.concatenate([x, x], axis=0).T
        u[:, n, :] = x
        f0[every8(n, 64), :] = jnp.where(low_half((64, 128)), x[:64], x[64:])

    pl.semaphore_wait(barrier, len(everyone))

    def exchange(app):
        copies = []
        for index, (other, start, stop, to) in enumerate(
            ((lower, 0, 32, 32), (upper, 32, 64, 0), (partner, 64, 128, 64))
        ):
            copy = pltpu.make_async_remote_copy(
                src_ref=sbuf.at[app, :, pl.ds(start, stop - start), :],
                dst_ref=rbuf.at[app, :, pl.ds(to, stop - start), :],
                send_sem=xsend.at[app, index],
                recv_sem=xrecv.at[app, index],
                device_id=place(other),
                device_id_type=MESH,
            )
            copy.start()
            copies.append(copy)
        return copies

    def reduce_start(which, stage, value):
        arsend[which, stage] = value
        first = sum(size - 1 for size in sizes[:stage])
        copies = []
        for index, other in enumerate(peers[stage]):
            copy = pltpu.make_async_remote_copy(
                src_ref=arsend.at[which, stage],
                dst_ref=arrecv.at[which, first + index],
                send_sem=asend.at[which, first + index],
                recv_sem=arecv.at[which, first + index],
                device_id=place(other),
                device_id_type=MESH,
            )
            copy.start()
            copies.append(copy)
        return copies

    def reduce_end(which, stage, copies):
        for copy in copies:
            copy.wait()
        total = arsend[which, stage]
        first = sum(size - 1 for size in sizes[:stage])
        for index in range(len(copies)):
            total = total + arrecv[which, first + index]
        return total

    def transpose_slots(app):
        def body(sp, carry):
            parts = [
                jnp.where(low8, u[frows_s[sp]], zero8),
                jnp.where(low8, zero8, u[frows_s[32 + sp]]),
                jnp.where(low8, u[crows_s[sp]], zero8),
                jnp.where(low8, zero8, u[crows_s[32 + sp]]),
            ]
            out = split_dot(dot, jnp.concatenate(parts, axis=0), tile_at(e, sp))
            put8(ps, sp, jnp.where(low8, out[0:8], out[16:24]))
            put8(ps, 32 + sp, jnp.where(low8, out[8:16], out[24:32]))
            return carry

        lax.fori_loop(0, 32, body, 0, unroll=4)
        for np in range(4):
            face, contact = pair(ps[every8(2 * np, 64), :], ps[every8(2 * np + 1, 64), :])
            sbuf[app, np, 0:64] = face
            sbuf[app, np, 64:128] = contact
        return exchange(app)

    def transpose_inner(field):
        def body(jp, carry):
            high, rest = split_wide(block8(field, jp))
            parts = [
                jnp.where(low8, high, zero8),
                jnp.where(low8, rest, zero8),
                jnp.where(low8, zero8, high),
                jnp.where(low8, zero8, rest),
            ]
            out = dot(jnp.concatenate(parts, axis=0).astype(BF16), tile_at(w, jp))
            x = out[0:8] + out[8:16]
            y = out[16:24] + out[24:32]
            put8(p01, jp, x[:, :128])
            put8(p23, jp, x[:, 128:])
            put8(p01, 64 + jp, y[:, :128])
            put8(p23, 64 + jp, y[:, 128:])
            return carry

        lax.fori_loop(0, 64, body, 0, unroll=4)

    def transpose_end(app, copies, result, send_app):
        for copy in copies:
            copy.wait()
        low = low_half((128, 128))
        for np in range(4):
            k0, k1 = pair(p01[every8(2 * np, 128), :], p01[every8(2 * np + 1, 128), :])
            k2, k3 = pair(p23[every8(2 * np, 128), :], p23[every8(2 * np + 1, 128), :])
            high, rest = split(jnp.concatenate([k0, k1, k2, k3], axis=0))
            z = dot(ohk[...], high) + dot(ohk[...], rest)
            high, rest = split(rbuf[app, np])
            z = z + (dot(ohs[...], high) + dot(ohs[...], rest))
            if send_app is not None:
                high, rest = split(z)
                sbuf[send_app, np] = dot(ohst[...], high) + dot(ohst[...], rest)
            other = swap(z)
            result[:, 2 * np, :] = jnp.where(low, z, other)
            result[:, 2 * np + 1, :] = jnp.where(low, other, z)
        if send_app is not None:
            return exchange(send_app)

    def forward_inner(field, result):
        def body(jp, carry):
            parts = []
            for j2 in range(2):
                j = j2 * 64 + jp
                v = [field[cols_s[k, j]] for k in range(4)]
                x = jnp.concatenate(
                    [jnp.where(low8, v[0], v[1]), jnp.where(low8, v[2], v[3])], axis=1
                )
                parts += list(split_wide(x))
            out = dot_nt(jnp.concatenate(parts, axis=0).astype(BF16), tile_at(w, jp))
            put8(result, jp, jnp.where(low8, out[0:8] + out[8:16], out[16:24] + out[24:32]))
            return carry

        lax.fori_loop(0, 64, body, 0, unroll=4)

    def forward_end(app, copies, result):
        for copy in copies:
            copy.wait()
        low = low_half((64, 128))
        for np in range(4):
            x = rbuf[app, np]
            face, contact = x[:64], x[64:]
            xf[every8(2 * np, 64), :] = jnp.where(low, face, 0.0)
            xf[every8(2 * np + 1, 64), :] = jnp.where(low, swap(face), 0.0)
            xf[every8(512 + 2 * np, 64), :] = jnp.where(low, 0.0, swap(contact))
            xf[every8(512 + 2 * np + 1, 64), :] = jnp.where(low, 0.0, contact)

        def body(sp, carry):
            parts = [block8(xf, sp + 32 * i) for i in range(4)]
            out = split_dot(dot_nt, jnp.concatenate(parts, axis=0), tile_at(e, sp))
            put8(uo, sp, jnp.where(low8, out[0:8], out[8:16]))
            put8(uo, 32 + sp, jnp.where(low8, out[16:24], out[24:32]))
            return carry

        lax.fori_loop(0, 32, body, 0, unroll=4)
        for np in range(4):
            s0, s1 = pair(uo[every8(2 * np, 64), :], uo[every8(2 * np + 1, 64), :])
            high, rest = split(jnp.concatenate([s0, s1], axis=0))
            y = dot(ohr[...], high) + dot(ohr[...], rest)
            n0, n1 = pair(y[:64], y[64:])
            result[every8(2 * np, 64), :] = result[every8(2 * np, 64), :] + n0
            result[every8(2 * np + 1, 64), :] = result[every8(2 * np + 1, 64), :] + n1

    def total(x):
        x = jnp.sum(x.reshape(-1, 8, 128), axis=0)
        return jnp.broadcast_to(jnp.sum(x, axis=1, keepdims=True), (8, 128))

    lane8 = lax.broadcasted_iota(jnp.int32, (8, 128), 1)

    def column(x, index):
        return jnp.broadcast_to(x[:, index : index + 1], (8, 128))

    def each(x, rows):
        return jnp.broadcast_to(x[None], (rows // 8, 8, 128)).reshape(rows, 128)

    copies = transpose_slots(0)
    transpose_inner(f0)
    copies = transpose_end(0, copies, z0, 1)
    forward_inner(z0, fw)
    zz = total(z0[...] * z0[...]) * 0.5
    forward_end(1, copies, fw)
    ww = total(fw[...] * fw[...])
    going = reduce_start(0, 0, jnp.where(lane8 < 64, zz, ww))
    spread(fw)
    copies = transpose_slots(2)
    going = reduce_start(0, 1, reduce_end(0, 0, going))
    transpose_inner(fw)
    going = reduce_start(0, 2, reduce_end(0, 1, going))
    copies = transpose_end(2, copies, q, 3)
    forward_inner(q, fs)
    sums = reduce_end(0, 2, going)
    zz0 = column(sums, 0)
    ww0 = column(sums, 64)
    alpha0 = zz0 / ww0
    forward_end(3, copies, fs)
    fs[...] = fw[...] - each(alpha0, 512) * fs[...]
    spread(fs)
    copies = transpose_slots(4)
    z1 = z0[...] - alpha0[None] * q[...]
    s1 = fs[...]
    zz = total(z1 * z1) * 0.5
    ss = total(s1 * s1)
    sw = total(s1 * fw[...])
    going = reduce_start(1, 0, jnp.where(lane8 < 32, zz, jnp.where(lane8 < 64, ss, sw)))
    transpose_inner(fs)
    going = reduce_start(1, 1, reduce_end(1, 0, going))
    transpose_end(4, copies, t, None)
    going = reduce_start(1, 2, reduce_end(1, 1, going))
    sums = reduce_end(1, 2, going)
    zz1 = column(sums, 0)
    beta = zz1 / zz0
    ww1 = column(sums, 32) + beta * (2.0 * column(sums, 64) + beta * ww0)
    alpha1 = zz1 / ww1

    a0, a1, b = (x[None] for x in (alpha0, alpha1, beta))
    z1 = z0[...] - a0 * q[...]
    t[...] = z1 - a1 * (t[...] + b * q[...])
    z0[...] = a0 * z0[...] + a1 * (z1 + b * z0[...])
    a0, a1, b = (each(x, 512) for x in (alpha0, alpha1, beta))
    f0[...] = f0[...] - a0 * fw[...] - a1 * (fs[...] + b * fw[...])

    low = low_half((128, 128))
    for np in range(4):
        for source, out in ((z0, adjoint), (t, normal)):
            x = jnp.where(low, source[:, 2 * np, :], source[:, 2 * np + 1, :]).T
            out[every8(2 * np, 64), :] = x[:64]
            out[every8(2 * np + 1, 64), :] = x[64:]
        top, bottom = pair(f0[every8(2 * np, 64), :], f0[every8(2 * np + 1, 64), :])
        x = jnp.concatenate([top, bottom], axis=0).T
        residual[every8(2 * np, 64), :] = x[:64]
        residual[every8(2 * np + 1, 64), :] = x[64:]


def shards(
    devices,
    rhs,
    inner_tiles,
    inner_cols,
    send_blocks,
    face_rows,
    face_counts,
    face_tiles,
    contact_send,
    contact_rows,
    contact_pair,
    contact_tiles,
):
    slot = jnp.arange(64, dtype=jnp.int32)
    paired_rows = jnp.sum(
        jnp.where(contact_pair[0][:, None] == slot[None, :], contact_rows[:, None], 0), axis=0
    )
    sends = jnp.concatenate([send_blocks, contact_send])[None]
    rows = jnp.concatenate(
        [face_rows[:32], paired_rows[:32], face_rows[32:], paired_rows[32:]]
    )[None]
    smem = pl.BlockSpec(memory_space=pltpu.SMEM)
    vmem = pl.BlockSpec(memory_space=pltpu.VMEM)
    copies = sum(size - 1 for size in stage_sizes(devices))
    out = jax.ShapeDtypeStruct((512, 128), F32)
    outs = pl.pallas_call(
        functools.partial(kernel, devices),
        out_shape=[out] * 3,
        in_specs=[smem] * 4 + [vmem] * 8,
        out_specs=[vmem] * 3,
        scratch_shapes=[
            pltpu.VMEM((8192, 128), F32),
            pltpu.VMEM((8192, 128), F32),
            pltpu.VMEM((8192, 256), BF16),
            pltpu.VMEM((4096, 128), F32),
            pltpu.VMEM((4096, 128), BF16),
            pltpu.VMEM((128, 512), BF16),
            pltpu.VMEM((128, 128), BF16),
            pltpu.VMEM((128, 128), BF16),
            pltpu.VMEM((128, 128), BF16),
            pltpu.VMEM((1024, 128), F32),
            pltpu.VMEM((1024, 128), F32),
            pltpu.VMEM((128, 8, 128), F32),
            pltpu.VMEM((128, 8, 128), F32),
            pltpu.VMEM((128, 8, 128), F32),
            pltpu.VMEM((512, 128), F32),
            pltpu.VMEM((512, 128), F32),
            pltpu.VMEM((512, 128), F32),
            pltpu.VMEM((128, 8, 128), F32),
            pltpu.VMEM((1024, 128), F32),
            pltpu.VMEM((512, 128), F32),
            pltpu.VMEM((512, 128), F32),
            pltpu.VMEM((APPS, 4, 128, 128), F32),
            pltpu.VMEM((APPS, 4, 128, 128), F32),
            pltpu.VMEM((2, 3, 8, 128), F32),
            pltpu.VMEM((2, copies, 8, 128), F32),
            pltpu.SemaphoreType.DMA((APPS, 3)),
            pltpu.SemaphoreType.DMA((APPS, 3)),
            pltpu.SemaphoreType.DMA((2, copies)),
            pltpu.SemaphoreType.DMA((2, copies)),
        ],
        compiler_params=pltpu.CompilerParams(
            collective_id=0, has_side_effects=True, vmem_limit_bytes=56 * 1024 * 1024
        ),
    )(
        inner_cols,
        face_rows,
        paired_rows,
        face_counts,
        rhs.reshape(512, 128),
        inner_tiles,
        inner_cols,
        sends,
        rows,
        contact_pair,
        face_tiles,
        contact_tiles,
    )
    return tuple(x.reshape(64, 8, 128) for x in outs)


def solution(mesh):
    both = ("dom", "sub")
    field = P(None, None, both)
    devices = 1
    for axis in both:
        devices *= mesh.shape[axis]
    return jax.shard_map(
        functools.partial(shards, devices),
        mesh=mesh,
        in_specs=(
            field,
            P(None, None, None, both),
            P(None, both),
            P(both),
            P(both),
            P(both, None),
            field,
            P(both),
            P(both),
            P(both, None),
            field,
        ),
        out_specs=(field,) * 3,
        check_vma=False,
    )
```

```python
import functools

import jax
import jax.numpy as jnp
from jax import lax
from jax.experimental import pallas as pl
from jax.experimental.pallas import tpu as pltpu
from jax.sharding import PartitionSpec as P

F32 = jnp.float32
BF16 = jnp.bfloat16
APPS = 5
MESH = pl.DeviceIdType.MESH
NT = (((1,), (1,)), ((), ()))


def stage_sizes(devices):
    bits = devices.bit_length() - 1
    first = min(3, bits - 2)
    second = min(3, bits - first - 1)
    return (1 << first, 1 << second, 1 << (bits - first - second))


def low_half(shape):
    return lax.broadcasted_iota(jnp.int32, shape, 1) < 64


def swap(x):
    return pltpu.roll(x, 64, 1)


def pair(x, y):
    low = low_half(x.shape)
    return jnp.where(low, x, swap(y)), jnp.where(low, swap(x), y)


def split(x):
    high = x.astype(BF16)
    return high, (x - high.astype(F32)).astype(BF16)


def split_wide(x):
    high = x.astype(BF16).astype(F32)
    return high, x - high


def dot(a, b):
    return jnp.dot(a, b, preferred_element_type=F32)


def dot_nt(a, b):
    return lax.dot_general(a, b, NT, preferred_element_type=F32)


def split_dot(product, a, b):
    rows = a.shape[0]
    out = product(jnp.concatenate(split(a), axis=0), b)
    return out[:rows] + out[rows:]


def block8(ref, index):
    return ref[pl.ds(pl.multiple_of(index * 8, 8), 8), :]


def put8(ref, index, value):
    ref[pl.ds(pl.multiple_of(index * 8, 8), 8), :] = value


def every8(first, count):
    return pl.ds(first, count, stride=8)


def kernel(
    devices,
    cols_s,
    frows_s,
    crows_s,
    counts_s,
    rhs,
    cols_v,
    send_v,
    csend_v,
    frows_v,
    crows_v,
    pair_v,
    tiles_h,
    ftiles_h,
    ctiles_h,
    adjoint,
    residual,
    normal,
    tiles,
    ftiles,
    ctiles,
    wf0,
    wf1,
    w,
    ef,
    e,
    ohk,
    ohs,
    ohst,
    ohr,
    p01,
    p23,
    zs,
    z0,
    q,
    t,
    f0,
    fw,
    fs,
    u,
    xf,
    ps,
    uo,
    sbuf,
    rbuf,
    arsend,
    arrecv,
    xsend,
    xrecv,
    asend,
    arecv,
    fetched,
):
    fetches = [
        pltpu.make_async_copy(source, target, fetched.at[index])
        for index, (source, target) in enumerate(
            ((ftiles_h, ftiles), (ctiles_h, ctiles), (tiles_h, tiles))
        )
    ]
    for fetch in fetches:
        fetch.start()
    me = lax.axis_index("dom") * 2 + lax.axis_index("sub")
    sizes = stage_sizes(devices)

    def place(index):
        return (index // 2, lax.rem(index, 2))

    lower = lax.rem(me + devices - 1, devices)
    upper = lax.rem(me + 1, devices)
    partner = lax.rem(me + devices // 2, devices)

    def group_peers(stage):
        stride = 1
        for size in sizes[:stage]:
            stride *= size
        size = sizes[stage]
        mine = lax.rem(me // stride, size)
        return [me + (lax.rem(mine + i, size) - mine) * stride for i in range(1, size)]

    peers = [group_peers(stage) for stage in range(3)]
    everyone = [lower, upper, partner] + peers[0] + peers[1] + peers[2]

    barrier = pltpu.get_barrier_semaphore()
    for other in everyone:
        pl.semaphore_signal(barrier, inc=1, device_id=place(other), device_id_type=MESH)

    row_id = lax.broadcasted_iota(jnp.int32, (128, 128), 0)
    lane_id = lax.broadcasted_iota(jnp.int32, (128, 128), 1)
    for half in range(2):
        for k in range(4):
            at = half * 512 + k * 128
            ohk[:, at : at + 128] = jnp.where(cols_v[k : k + 1, :] == row_id, 1.0, 0.0).astype(BF16)
    picks = jnp.concatenate([send_v[...], csend_v[...]], axis=1) == row_id
    picks = jnp.where(picks, 1.0, 0.0)
    ohs[...] = jnp.concatenate([picks.astype(BF16)] * 2, axis=1)
    picks = picks.T.astype(BF16)
    ohst[...] = jnp.concatenate([picks] * 2, axis=1)
    picks = jnp.concatenate([frows_v[...], crows_v[...]], axis=1) == row_id
    picks = jnp.where(picks, 1.0, 0.0).astype(BF16)
    ohr[...] = jnp.concatenate([picks] * 2, axis=1)
    eye = jnp.where(row_id == lane_id, 1.0, 0.0).astype(BF16)

    def prepare(a, carry):
        for half, out in ((0, wf0), (1, wf1)):
            x = tiles[2 * half : 2 * half + 2, a].reshape(128, 128)
            x = turned(half, x)
            out[pl.ds(a, 64, stride=128), :] = x[:64]
            out[pl.ds(64 + a, 64, stride=128), :] = x[64:]
        return carry

    def turned(half, x):
        return x.astype(F32).T if half else dot_nt(eye, x)

    def pack(i, carry):
        at = pl.ds(pl.multiple_of(i * 128, 128), 128)
        w[at, 0:128] = wf0[at, :].astype(BF16)
        w[at, 128:256] = wf1[at, :].astype(BF16)
        return carry

    def prepare_inner():
        fetches[2].wait()
        lax.fori_loop(0, 64, prepare, 0, unroll=8)
        lax.fori_loop(0, 64, pack, 0, unroll=4)

    for n in range(8):
        x = rhs[every8(n, 64), :]
        x = jnp.concatenate([x, x], axis=0).T
        u[:, n, :] = x
        f0[every8(n, 64), :] = jnp.where(low_half((64, 128)), x[:64], x[64:])

    slot = lax.broadcasted_iota(jnp.int32, (64, 64), 0)
    other_slot = lax.broadcasted_iota(jnp.int32, (64, 64), 1)
    side_a = (slot < 32) & (slot < counts_s[0, 0])
    side_b = (slot >= 32) & (slot - 32 < counts_s[0, 1])
    face_pick = jnp.where((slot == other_slot) & (side_a | side_b), 1.0, 0.0)
    contact_pick = jnp.where(pair_v[...] == slot, 1.0, 0.0)
    slot_pick = jnp.concatenate([face_pick, contact_pick], axis=0).astype(BF16)

    def prepare_slots(i, carry):
        parts = []
        for n in range(4):
            parts += [ftiles[4 * i + n], ctiles[4 * i + n]]
        x = dot_nt(slot_pick, jnp.concatenate(parts, axis=0))
        for n in range(4):
            a = 4 * i + n
            y = x[:, 128 * n : 128 * n + 128]
            y = jnp.where(low_half((64, 128)), y[:64], y[64:])
            ef[pl.ds(a, 32, stride=128), :] = y[:32]
            ef[pl.ds(64 + a, 32, stride=128), :] = y[32:]
        return carry

    for fetch in fetches[:2]:
        fetch.wait()
    lax.fori_loop(0, 16, prepare_slots, 0, unroll=2)

    def pack_slots(i, carry):
        at = pl.ds(pl.multiple_of(i * 128, 128), 128)
        e[at, :] = ef[at, :].astype(BF16)
        return carry

    lax.fori_loop(0, 32, pack_slots, 0, unroll=4)

    def tile_at(ref, index):
        return ref[pl.ds(pl.multiple_of(index * 128, 128), 128), :]

    low8 = low_half((8, 128))
    zero8 = jnp.zeros((8, 128), F32)

    def spread(field):
        x = field[...]
        y = swap(x)
        low = low_half(x.shape)
        u[0:64] = jnp.where(low, x, y).reshape(64, 8, 128)
        u[64:128] = jnp.where(low, y, x).reshape(64, 8, 128)

    pl.semaphore_wait(barrier, len(everyone))

    def exchange(app):
        copies = []
        for index, (other, start, stop, to) in enumerate(
            ((lower, 0, 32, 32), (upper, 32, 64, 0), (partner, 64, 128, 64))
        ):
            copy = pltpu.make_async_remote_copy(
                src_ref=sbuf.at[app, :, pl.ds(start, stop - start), :],
                dst_ref=rbuf.at[app, :, pl.ds(to, stop - start), :],
                send_sem=xsend.at[app, index],
                recv_sem=xrecv.at[app, index],
                device_id=place(other),
                device_id_type=MESH,
            )
            copy.start()
            copies.append(copy)
        return copies

    def reduce_start(which, stage, value):
        arsend[which, stage] = value
        first = sum(size - 1 for size in sizes[:stage])
        copies = []
        for index, other in enumerate(peers[stage]):
            copy = pltpu.make_async_remote_copy(
                src_ref=arsend.at[which, stage],
                dst_ref=arrecv.at[which, first + index],
                send_sem=asend.at[which, first + index],
                recv_sem=arecv.at[which, first + index],
                device_id=place(other),
                device_id_type=MESH,
            )
            copy.start()
            copies.append(copy)
        return copies

    def reduce_end(which, stage, copies):
        for copy in copies:
            copy.wait()
        total = arsend[which, stage]
        first = sum(size - 1 for size in sizes[:stage])
        for index in range(len(copies)):
            total = total + arrecv[which, first + index]
        return total

    def transpose_slots(app):
        def body(sp, carry):
            parts = [
                jnp.where(low8, u[frows_s[sp]], zero8),
                jnp.where(low8, zero8, u[frows_s[32 + sp]]),
                jnp.where(low8, u[crows_s[sp]], zero8),
                jnp.where(low8, zero8, u[crows_s[32 + sp]]),
            ]
            out = split_dot(dot, jnp.concatenate(parts, axis=0), tile_at(e, sp))
            put8(ps, sp, jnp.where(low8, out[0:8], out[16:24]))
            put8(ps, 32 + sp, jnp.where(low8, out[8:16], out[24:32]))
            return carry

        lax.fori_loop(0, 32, body, 0, unroll=8)
        for np in range(4):
            face, contact = pair(ps[every8(2 * np, 64), :], ps[every8(2 * np + 1, 64), :])
            sbuf[app, np, 0:64] = face
            sbuf[app, np, 64:128] = contact
        return exchange(app)

    def transpose_inner(field):
        def body(jp, carry):
            high, rest = split_wide(block8(field, jp))
            parts = [
                jnp.where(low8, high, zero8),
                jnp.where(low8, rest, zero8),
                jnp.where(low8, zero8, high),
                jnp.where(low8, zero8, rest),
            ]
            out = dot(jnp.concatenate(parts, axis=0).astype(BF16), tile_at(w, jp))
            x = out[0:8] + out[8:16]
            y = out[16:24] + out[24:32]
            put8(p01, jp, x[:, :128])
            put8(p23, jp, x[:, 128:])
            put8(p01, 64 + jp, y[:, :128])
            put8(p23, 64 + jp, y[:, 128:])
            return carry

        lax.fori_loop(0, 64, body, 0, unroll=8)

    def halves(parts):
        x = jnp.concatenate(parts, axis=1)
        return jnp.concatenate(split(x), axis=0)

    def transpose_end(app, copies, result, send_app):
        parts = []
        for np in range(4):
            k0, k1 = pair(p01[every8(2 * np, 128), :], p01[every8(2 * np + 1, 128), :])
            k2, k3 = pair(p23[every8(2 * np, 128), :], p23[every8(2 * np + 1, 128), :])
            parts.append(jnp.concatenate([k0, k1, k2, k3], axis=0))
        zs[...] = dot(ohk[...], halves(parts))
        for copy in copies:
            copy.wait()
        low = low_half((128, 128))
        z = zs[...] + dot(ohs[...], halves([rbuf[app, np] for np in range(4)]))
        if send_app is not None:
            x = dot(ohst[...], jnp.concatenate(split(z), axis=0))
            for np in range(4):
                sbuf[send_app, np] = x[:, 128 * np : 128 * np + 128]
            copies = exchange(send_app)
        for np in range(4):
            x = z[:, 128 * np : 128 * np + 128]
            other = swap(x)
            result[:, 2 * np, :] = jnp.where(low, x, other)
            result[:, 2 * np + 1, :] = jnp.where(low, other, x)
        return copies

    def forward_inner(field, result):
        def body(jp, carry):
            parts = []
            for j2 in range(2):
                j = j2 * 64 + jp
                v = [field[cols_s[k, j]] for k in range(4)]
                x = jnp.concatenate(
                    [jnp.where(low8, v[0], v[1]), jnp.where(low8, v[2], v[3])], axis=1
                )
                parts += list(split_wide(x))
            out = dot_nt(jnp.concatenate(parts, axis=0).astype(BF16), tile_at(w, jp))
            put8(result, jp, jnp.where(low8, out[0:8] + out[8:16], out[16:24] + out[24:32]))
            return carry

        lax.fori_loop(0, 64, body, 0, unroll=8)

    def forward_end(app, copies, result):
        for copy in copies:
            copy.wait()
        low = low_half((64, 128))
        for np in range(4):
            x = rbuf[app, np]
            face, contact = x[:64], x[64:]
            xf[every8(2 * np, 64), :] = jnp.where(low, face, 0.0)
            xf[every8(2 * np + 1, 64), :] = jnp.where(low, swap(face), 0.0)
            xf[every8(512 + 2 * np, 64), :] = jnp.where(low, 0.0, swap(contact))
            xf[every8(512 + 2 * np + 1, 64), :] = jnp.where(low, 0.0, contact)

        def body(sp, carry):
            parts = [block8(xf, sp + 32 * i) for i in range(4)]
            out = split_dot(dot_nt, jnp.concatenate(parts, axis=0), tile_at(e, sp))
            put8(uo, sp, jnp.where(low8, out[0:8], out[8:16]))
            put8(uo, 32 + sp, jnp.where(low8, out[16:24], out[24:32]))
            return carry

        lax.fori_loop(0, 32, body, 0, unroll=8)
        parts = []
        for np in range(4):
            s0, s1 = pair(uo[every8(2 * np, 64), :], uo[every8(2 * np + 1, 64), :])
            parts.append(jnp.concatenate([s0[:32], s1[:32], s0[32:], s1[32:]], axis=0))
        y = dot(ohr[...], halves(parts))
        sums = []
        for np in range(4):
            x = y[:, 128 * np : 128 * np + 128]
            for n, x in enumerate(pair(x[:64], x[64:])):
                sums.append(result[every8(2 * np + n, 64), :] + x)
        for n, x in enumerate(sums):
            result[every8(n, 64), :] = x

    def total(x):
        x = jnp.sum(x.reshape(-1, 8, 128), axis=0)
        return jnp.broadcast_to(jnp.sum(x, axis=1, keepdims=True), (8, 128))

    lane8 = lax.broadcasted_iota(jnp.int32, (8, 128), 1)

    def column(x, index):
        return jnp.broadcast_to(x[:, index : index + 1], (8, 128))

    def each(x, rows):
        return jnp.broadcast_to(x[None], (rows // 8, 8, 128)).reshape(rows, 128)

    copies = transpose_slots(0)
    prepare_inner()
    transpose_inner(f0)
    copies = transpose_end(0, copies, z0, 1)
    forward_inner(z0, fw)
    zz = total(z0[...] * z0[...]) * 0.5
    forward_end(1, copies, fw)
    ww = total(fw[...] * fw[...])
    going = reduce_start(0, 0, jnp.where(lane8 < 64, zz, ww))
    spread(fw)
    copies = transpose_slots(2)
    going = reduce_start(0, 1, reduce_end(0, 0, going))
    transpose_inner(fw)
    going = reduce_start(0, 2, reduce_end(0, 1, going))
    copies = transpose_end(2, copies, q, 3)
    forward_inner(q, fs)
    sums = reduce_end(0, 2, going)
    zz0 = column(sums, 0)
    ww0 = column(sums, 64)
    alpha0 = zz0 / ww0
    forward_end(3, copies, fs)
    s1 = fw[...] - each(alpha0, 512) * fs[...]
    fs[...] = s1
    z1 = z0[...] - alpha0[None] * q[...]
    zz = total(z1 * z1) * 0.5
    ss = total(s1 * s1)
    sw = total(s1 * fw[...])
    going = reduce_start(1, 0, jnp.where(lane8 < 32, zz, jnp.where(lane8 < 64, ss, sw)))
    spread(fs)
    copies = transpose_slots(4)
    transpose_inner(fs)
    going = reduce_start(1, 1, reduce_end(1, 0, going))
    transpose_end(4, copies, t, None)
    going = reduce_start(1, 2, reduce_end(1, 1, going))
    sums = reduce_end(1, 2, going)
    zz1 = column(sums, 0)
    beta = zz1 / zz0
    ww1 = column(sums, 32) + beta * (2.0 * column(sums, 64) + beta * ww0)
    alpha1 = zz1 / ww1

    a0, a1, b = (x[None] for x in (alpha0, alpha1, beta))
    z1 = z0[...] - a0 * q[...]
    t[...] = z1 - a1 * (t[...] + b * q[...])
    z0[...] = a0 * z0[...] + a1 * (z1 + b * z0[...])
    a0, a1, b = (each(x, 512) for x in (alpha0, alpha1, beta))
    f0[...] = f0[...] - a0 * fw[...] - a1 * (fs[...] + b * fw[...])

    low = low_half((128, 128))
    for np in range(4):
        at = slice(128 * np, 128 * np + 128)
        for source, out in ((z0, adjoint), (t, normal)):
            out[at] = jnp.where(low, source[:, 2 * np, :], source[:, 2 * np + 1, :])
        top, bottom = pair(f0[every8(2 * np, 64), :], f0[every8(2 * np + 1, 64), :])
        residual[at] = jnp.concatenate([top, bottom], axis=0)


def turn(*refs):
    for source, out in zip(refs[:3], refs[3:]):
        for np in range(4):
            x = source[128 * np : 128 * np + 128].T
            out[every8(2 * np, 64), :] = x[:64]
            out[every8(2 * np + 1, 64), :] = x[64:]


def shards(
    devices,
    rhs,
    inner_tiles,
    inner_cols,
    send_blocks,
    face_rows,
    face_counts,
    face_tiles,
    contact_send,
    contact_rows,
    contact_pair,
    contact_tiles,
):
    slot = jnp.arange(64, dtype=jnp.int32)
    paired_rows = jnp.sum(
        jnp.where(contact_pair[0][:, None] == slot[None, :], contact_rows[:, None], 0), axis=0
    )
    smem = pl.BlockSpec(memory_space=pltpu.SMEM)
    vmem = pl.BlockSpec(memory_space=pltpu.VMEM)
    copies = sum(size - 1 for size in stage_sizes(devices))
    out = jax.ShapeDtypeStruct((512, 128), F32)
    outs = pl.pallas_call(
        functools.partial(kernel, devices),
        out_shape=[out] * 3,
        in_specs=[smem] * 4 + [vmem] * 7 + [pl.BlockSpec(memory_space=pl.ANY)] * 3,
        out_specs=[vmem] * 3,
        scratch_shapes=[
            pltpu.VMEM(inner_tiles.shape, BF16),
            pltpu.VMEM(face_tiles.shape, BF16),
            pltpu.VMEM(contact_tiles.shape, BF16),
            pltpu.VMEM((8192, 128), F32),
            pltpu.VMEM((8192, 128), F32),
            pltpu.VMEM((8192, 256), BF16),
            pltpu.VMEM((4096, 128), F32),
            pltpu.VMEM((4096, 128), BF16),
            pltpu.VMEM((128, 1024), BF16),
            pltpu.VMEM((128, 256), BF16),
            pltpu.VMEM((128, 256), BF16),
            pltpu.VMEM((128, 256), BF16),
            pltpu.VMEM((1024, 128), F32),
            pltpu.VMEM((1024, 128), F32),
            pltpu.VMEM((128, 512), F32),
            pltpu.VMEM((128, 8, 128), F32),
            pltpu.VMEM((128, 8, 128), F32),
            pltpu.VMEM((128, 8, 128), F32),
            pltpu.VMEM((512, 128), F32),
            pltpu.VMEM((512, 128), F32),
            pltpu.VMEM((512, 128), F32),
            pltpu.VMEM((128, 8, 128), F32),
            pltpu.VMEM((1024, 128), F32),
            pltpu.VMEM((512, 128), F32),
            pltpu.VMEM((512, 128), F32),
            pltpu.VMEM((APPS, 4, 128, 128), F32),
            pltpu.VMEM((APPS, 4, 128, 128), F32),
            pltpu.VMEM((2, 3, 8, 128), F32),
            pltpu.VMEM((2, copies, 8, 128), F32),
            pltpu.SemaphoreType.DMA((APPS, 3)),
            pltpu.SemaphoreType.DMA((APPS, 3)),
            pltpu.SemaphoreType.DMA((2, copies)),
            pltpu.SemaphoreType.DMA((2, copies)),
            pltpu.SemaphoreType.DMA((3,)),
        ],
        compiler_params=pltpu.CompilerParams(
            collective_id=0, has_side_effects=True, vmem_limit_bytes=56 * 1024 * 1024
        ),
    )(
        inner_cols,
        face_rows,
        paired_rows,
        face_counts,
        rhs.reshape(512, 128),
        inner_cols,
        send_blocks[None],
        contact_send[None],
        face_rows[None],
        paired_rows[None],
        contact_pair,
        inner_tiles,
        face_tiles,
        contact_tiles,
    )
    outs = pl.pallas_call(
        turn, out_shape=[out] * 3, in_specs=[vmem] * 3, out_specs=[vmem] * 3
    )(*outs)
    return tuple(x.reshape(64, 8, 128) for x in outs)


def solution(mesh):
    both = ("dom", "sub")
    field = P(None, None, both)
    devices = 1
    for axis in both:
        devices *= mesh.shape[axis]
    return jax.shard_map(
        functools.partial(shards, devices),
        mesh=mesh,
        in_specs=(
            field,
            P(None, None, None, both),
            P(None, both),
            P(both),
            P(both),
            P(both, None),
            field,
            P(both),
            P(both),
            P(both, None),
            field,
        ),
        out_specs=(field,) * 3,
        check_vma=False,
    )
```

```python
import functools

import jax
import jax.numpy as jnp
from jax import lax
from jax.experimental import pallas as pl
from jax.experimental.pallas import tpu as pltpu
from jax.sharding import PartitionSpec as P

F32 = jnp.float32
BF16 = jnp.bfloat16
APPS = 5
MESH = pl.DeviceIdType.MESH
PAD = 136
NT = (((1,), (1,)), ((), ()))


def stage_sizes(devices):
    bits = devices.bit_length() - 1
    first = min(3, bits - 2)
    second = min(3, bits - first - 1)
    return (1 << first, 1 << second, 1 << (bits - first - second))


def low_half(shape):
    return lax.broadcasted_iota(jnp.int32, shape, 1) < 64


def swap(x):
    return pltpu.roll(x, 64, 1)


def pair(x, y):
    low = low_half(x.shape)
    return jnp.where(low, x, swap(y)), jnp.where(low, swap(x), y)


def split(x):
    high = x.astype(BF16)
    return high, (x - high.astype(F32)).astype(BF16)


def split_wide(x):
    high = x.astype(BF16).astype(F32)
    return high, x - high


def dot(a, b):
    return jnp.dot(a, b, preferred_element_type=F32)


def dot_nt(a, b):
    return lax.dot_general(a, b, NT, preferred_element_type=F32)


def split_dot(product, a, b):
    rows = a.shape[0]
    out = product(jnp.concatenate(split(a), axis=0), b)
    return out[:rows] + out[rows:]


def block8(ref, index):
    return ref[pl.ds(pl.multiple_of(index * 8, 8), 8), :]


def put8(ref, index, value):
    ref[pl.ds(pl.multiple_of(index * 8, 8), 8), :] = value


def every8(first, count):
    return pl.ds(first, count, stride=8)


def kernel(
    devices,
    cols_s,
    frows_s,
    crows_s,
    counts_s,
    rhs,
    cols_v,
    send_v,
    csend_v,
    frows_v,
    crows_v,
    pair_v,
    tiles_h,
    ftiles_h,
    ctiles_h,
    adjoint,
    residual,
    normal,
    tiles,
    ftiles,
    ctiles,
    wf0,
    wf1,
    w,
    ef,
    e,
    ohk,
    ohs,
    ohst,
    ohr,
    p01,
    p23,
    zs,
    z0,
    q,
    f0,
    fw,
    fs,
    u,
    xf,
    ps,
    uo,
    sbuf,
    rbuf,
    arsend,
    arrecv,
    xsend,
    xrecv,
    asend,
    arecv,
    fetched,
):
    fetches = [
        pltpu.make_async_copy(source, target, fetched.at[index])
        for index, (source, target) in enumerate(
            ((ftiles_h, ftiles), (ctiles_h, ctiles), (tiles_h, tiles))
        )
    ]
    for fetch in fetches:
        fetch.start()
    me = lax.axis_index("dom") * 2 + lax.axis_index("sub")
    sizes = stage_sizes(devices)

    def place(index):
        return (index // 2, lax.rem(index, 2))

    lower = lax.rem(me + devices - 1, devices)
    upper = lax.rem(me + 1, devices)
    partner = lax.rem(me + devices // 2, devices)

    def group_peers(stage):
        stride = 1
        for size in sizes[:stage]:
            stride *= size
        size = sizes[stage]
        mine = lax.rem(me // stride, size)
        return [me + (lax.rem(mine + i, size) - mine) * stride for i in range(1, size)]

    peers = [group_peers(stage) for stage in range(3)]
    ar_first = [sum(size - 1 for size in sizes[:stage]) for stage in range(3)]
    everyone = [lower, upper, partner] + peers[0] + peers[1] + peers[2]

    barrier = pltpu.get_barrier_semaphore()
    for other in everyone:
        pl.semaphore_signal(barrier, inc=1, device_id=place(other), device_id_type=MESH)

    row_id = lax.broadcasted_iota(jnp.int32, (128, 128), 0)
    for half in range(2):
        for k in range(4):
            at = half * 512 + k * 128
            ohk[:, at : at + 128] = jnp.where(cols_v[k : k + 1, :] == row_id, 1.0, 0.0).astype(BF16)
    picks = jnp.concatenate([send_v[...], csend_v[...]], axis=1) == row_id
    picks = jnp.where(picks, 1.0, 0.0)
    ohs[...] = jnp.concatenate([picks.astype(BF16)] * 2, axis=1)
    picks = picks.T.astype(BF16)
    ohst[...] = jnp.concatenate([picks] * 2, axis=1)
    picks = jnp.concatenate([frows_v[...], crows_v[...]], axis=1) == row_id
    picks = jnp.where(picks, 1.0, 0.0).astype(BF16)
    ohr[...] = jnp.concatenate([picks] * 2, axis=1)

    def prepare(a, carry):
        for half, out in ((0, wf0), (1, wf1)):
            x = tiles[2 * half : 2 * half + 2, a].reshape(128, 128)
            x = x.astype(F32).T
            out[pl.ds(a, 64, stride=PAD), :] = x[:64]
            out[pl.ds(64 + a, 64, stride=PAD), :] = x[64:]
        return carry

    def pack(i, carry):
        at = pl.ds(pl.multiple_of(i * 128, 128), 128)
        padded = pl.ds(pl.multiple_of(i * PAD, 8), 128)
        w[at, 0:128] = wf0[padded, :].astype(BF16)
        w[at, 128:256] = wf1[padded, :].astype(BF16)
        return carry

    def prepare_inner():
        fetches[2].wait()
        lax.fori_loop(0, 64, prepare, 0, unroll=8)
        lax.fori_loop(0, 64, pack, 0, unroll=4)

    for n in range(8):
        x = rhs[every8(n, 64), :]
        x = jnp.concatenate([x, x], axis=0).T
        u[:, n, :] = x
        f0[every8(n, 64), :] = jnp.where(low_half((64, 128)), x[:64], x[64:])

    slot = lax.broadcasted_iota(jnp.int32, (64, 64), 0)
    other_slot = lax.broadcasted_iota(jnp.int32, (64, 64), 1)
    side_a = (slot < 32) & (slot < counts_s[0, 0])
    side_b = (slot >= 32) & (slot - 32 < counts_s[0, 1])
    face_pick = jnp.where((slot == other_slot) & (side_a | side_b), 1.0, 0.0)
    contact_pick = jnp.where(pair_v[...] == slot, 1.0, 0.0)
    slot_picks = (face_pick.astype(BF16), contact_pick.astype(BF16))

    def prepare_slots(i, carry):
        for kind, source in enumerate((ftiles, ctiles)):
            parts = []
            for n in range(4):
                parts += [source[4 * i + n]] * 2
            x = dot_nt(slot_picks[kind], jnp.concatenate(parts, axis=0))
            for n in range(4):
                y = x[:, 128 * n : 128 * n + 128]
                for s2 in range(2):
                    at = 32 * s2
                    ef[pl.ds(kind * 16 * PAD + s2 * 64 + 4 * i + n, 16, stride=PAD), :] = jnp.where(
                        low_half((16, 128)), y[at : at + 16], y[at + 16 : at + 32]
                    )
        return carry

    for fetch in fetches[:2]:
        fetch.wait()
    lax.fori_loop(0, 16, prepare_slots, 0, unroll=2)

    def pack_slots(i, carry):
        at = pl.ds(pl.multiple_of(i * 128, 128), 128)
        e[at, :] = ef[pl.ds(pl.multiple_of(i * PAD, 8), 128), :].astype(BF16)
        return carry

    lax.fori_loop(0, 32, pack_slots, 0, unroll=4)

    def tile_at(ref, index):
        return ref[pl.ds(pl.multiple_of(index * 128, 128), 128), :]

    low8 = low_half((8, 128))
    zero8 = jnp.zeros((8, 128), F32)

    def spread(field):
        x = field[...]
        y = swap(x)
        low = low_half(x.shape)
        u[0:64] = jnp.where(low, x, y).reshape(64, 8, 128)
        u[64:128] = jnp.where(low, y, x).reshape(64, 8, 128)


    routes = ((lower, 0, 32, 32), (upper, 32, 64, 0), (partner, 64, 128, 64))

    def exchange(app, kind):
        copies = []
        for index in ((0, 1), (2,))[kind]:
            other, start, stop, to = routes[index]
            copy = pltpu.make_async_remote_copy(
                src_ref=sbuf.at[app, :, pl.ds(start, stop - start), :],
                dst_ref=rbuf.at[app, :, pl.ds(to, stop - start), :],
                send_sem=xsend.at[app, index],
                recv_sem=xrecv.at[app, index],
                device_id=place(other),
                device_id_type=MESH,
            )
            copy.start()
            copies.append(copy)
        return copies

    def reduce_start(which, step, value):
        stage = (1, 0, 2)[step]
        arsend[which, stage] = value
        for index, other in enumerate(peers[stage]):
            pltpu.make_async_remote_copy(
                src_ref=arsend.at[which, stage],
                dst_ref=arrecv.at[which, ar_first[stage] + index],
                send_sem=asend.at[which, stage],
                recv_sem=arecv.at[which, stage],
                device_id=place(other),
                device_id_type=MESH,
            ).start()

    def reduce_end(which, step):
        stage = (1, 0, 2)[step]
        arrived = arrecv.at[which, pl.ds(ar_first[stage], len(peers[stage]))]
        pltpu.make_async_copy(arrived, arrived, arecv.at[which, stage]).wait()
        pltpu.make_async_copy(arrived, arrived, asend.at[which, stage]).wait()
        total = arsend[which, stage]
        for index in range(len(peers[stage])):
            total = total + arrecv[which, ar_first[stage] + index]
        return total

    def transpose_slots(app):
        copies = []
        for kind, rows in enumerate((frows_s, crows_s)):

            def body(tp, carry):
                parts = []
                for h in range(2):
                    parts.append(jnp.where(low8, u[rows[16 * h + tp]], zero8))
                    parts.append(jnp.where(low8, zero8, u[rows[32 + 16 * h + tp]]))
                out = split_dot(dot, jnp.concatenate(parts, axis=0), tile_at(e, 16 * kind + tp))
                put8(ps, 32 * kind + tp, jnp.where(low8, out[0:8], out[16:24]))
                put8(ps, 32 * kind + 16 + tp, jnp.where(low8, out[8:16], out[24:32]))
                return carry

            lax.fori_loop(0, 16, body, 0, unroll=16)
            for np in range(4):
                at = 256 * kind + 2 * np
                x, y = pair(ps[every8(at, 32), :], ps[every8(at + 1, 32), :])
                sbuf[app, np, 64 * kind : 64 * kind + 64] = jnp.concatenate(
                    [x[:16], y[:16], x[16:], y[16:]], axis=0
                )
            if app == 0 and kind == 0:
                pl.semaphore_wait(barrier, len(everyone))
            copies += exchange(app, kind)
        return copies

    def transpose_inner(field):
        def body(jp, carry):
            high, rest = split_wide(block8(field, jp))
            parts = [
                jnp.where(low8, high, zero8),
                jnp.where(low8, rest, zero8),
                jnp.where(low8, zero8, high),
                jnp.where(low8, zero8, rest),
            ]
            out = dot(jnp.concatenate(parts, axis=0).astype(BF16), tile_at(w, jp))
            x = out[0:8] + out[8:16]
            y = out[16:24] + out[24:32]
            put8(p01, jp, x[:, :128])
            put8(p23, jp, x[:, 128:])
            put8(p01, 64 + jp, y[:, :128])
            put8(p23, 64 + jp, y[:, 128:])
            return carry

        lax.fori_loop(0, 64, body, 0, unroll=8)

    def halves(parts):
        x = jnp.concatenate(parts, axis=1)
        return jnp.concatenate(split(x), axis=0)

    def transpose_end(app, copies, result, send_app):
        parts = []
        for np in range(4):
            k0, k1 = pair(p01[every8(2 * np, 128), :], p01[every8(2 * np + 1, 128), :])
            k2, k3 = pair(p23[every8(2 * np, 128), :], p23[every8(2 * np + 1, 128), :])
            parts.append(jnp.concatenate([k0, k1, k2, k3], axis=0))
        zs[...] = dot(ohk[...], halves(parts))
        for copy in copies:
            copy.wait()
        low = low_half((128, 128))
        z = zs[...] + dot(ohs[...], halves([rbuf[app, np] for np in range(4)]))
        if send_app is not None:
            x = dot(ohst[...], jnp.concatenate(split(z), axis=0))
            for np in range(4):
                sbuf[send_app, np] = x[:, 128 * np : 128 * np + 128]
            copies = exchange(send_app, 0) + exchange(send_app, 1)
        for np in range(4):
            x = z[:, 128 * np : 128 * np + 128]
            if result is None:
                p01[128 * np : 128 * np + 128] = x
            else:
                other = swap(x)
                result[:, 2 * np, :] = jnp.where(low, x, other)
                result[:, 2 * np + 1, :] = jnp.where(low, other, x)
        return copies

    def forward_inner(field, result):
        def body(jp, carry):
            parts = []
            for j2 in range(2):
                j = j2 * 64 + jp
                v = [field[cols_s[k, j]] for k in range(4)]
                x = jnp.concatenate(
                    [jnp.where(low8, v[0], v[1]), jnp.where(low8, v[2], v[3])], axis=1
                )
                parts += list(split_wide(x))
            out = dot_nt(jnp.concatenate(parts, axis=0).astype(BF16), tile_at(w, jp))
            put8(result, jp, jnp.where(low8, out[0:8] + out[8:16], out[16:24] + out[24:32]))
            return carry

        lax.fori_loop(0, 64, body, 0, unroll=8)

    def forward_end(app, copies, result):
        low = low_half((64, 128))
        first = lax.rem(lax.broadcasted_iota(jnp.int32, (64, 128), 0) // 16, 2) == 0
        mine = low == first
        for kind in (1, 0):
            for copy in (copies[:2], copies[2:])[kind]:
                copy.wait()
            for np in range(4):
                x = rbuf[app, np, 64 * kind : 64 * kind + 64]
                y = swap(x)
                at = 512 * kind + 2 * np
                xf[every8(at, 64), :] = jnp.where(mine, jnp.where(first, x, y), 0.0)
                xf[every8(at + 1, 64), :] = jnp.where(mine, jnp.where(first, y, x), 0.0)

            def body(tp, carry):
                parts = []
                for h in range(2):
                    for s2 in range(2):
                        parts.append(block8(xf, 64 * kind + 32 * s2 + 16 * h + tp))
                tile = tile_at(e, 16 * kind + tp)
                out = split_dot(dot_nt, jnp.concatenate(parts, axis=0), tile)
                put8(uo, 32 * kind + tp, jnp.where(low8, out[0:8], out[8:16]))
                put8(uo, 32 * kind + 16 + tp, jnp.where(low8, out[16:24], out[24:32]))
                return carry

            lax.fori_loop(0, 16, body, 0, unroll=16)
        parts = []
        for np in range(4):
            s0, s1 = pair(uo[every8(2 * np, 64), :], uo[every8(2 * np + 1, 64), :])
            parts.append(jnp.concatenate([s0[:32], s1[:32], s0[32:], s1[32:]], axis=0))
        y = dot(ohr[...], halves(parts))
        sums = []
        for np in range(4):
            x = y[:, 128 * np : 128 * np + 128]
            for n, x in enumerate(pair(x[:64], x[64:])):
                sums.append(result[every8(2 * np + n, 64), :] + x)
        for n, x in enumerate(sums):
            result[every8(n, 64), :] = x

    def total(x):
        x = jnp.sum(x.reshape(-1, 8, 128), axis=0)
        return jnp.broadcast_to(jnp.sum(x, axis=1, keepdims=True), (8, 128))

    lane8 = lax.broadcasted_iota(jnp.int32, (8, 128), 1)

    def column(x, index):
        return jnp.broadcast_to(x[:, index : index + 1], (8, 128))

    def each(x, rows):
        return jnp.broadcast_to(x[None], (rows // 8, 8, 128)).reshape(rows, 128)

    copies = transpose_slots(0)
    prepare_inner()
    transpose_inner(f0)
    copies = transpose_end(0, copies, z0, 1)
    forward_inner(z0, fw)
    zz = total(z0[...] * z0[...]) * 0.5
    forward_end(1, copies, fw)
    ww = total(fw[...] * fw[...])
    reduce_start(0, 0, jnp.where(lane8 < 64, zz, ww))
    spread(fw)
    copies = transpose_slots(2)
    transpose_inner(fw)
    reduce_start(0, 1, reduce_end(0, 0))
    copies = transpose_end(2, copies, q, 3)
    forward_inner(q, fs)
    reduce_start(0, 2, reduce_end(0, 1))
    forward_end(3, copies, fs)
    sums = reduce_end(0, 2)
    zz0 = column(sums, 0)
    ww0 = column(sums, 64)
    alpha0 = zz0 / ww0
    s1 = fw[...] - each(alpha0, 512) * fs[...]
    fs[...] = s1
    z1 = z0[...] - alpha0[None] * q[...]
    zz = total(z1 * z1) * 0.5
    ss = total(s1 * s1)
    sw = total(s1 * fw[...])
    reduce_start(1, 0, jnp.where(lane8 < 32, zz, jnp.where(lane8 < 64, ss, sw)))
    spread(fs)
    copies = transpose_slots(4)
    transpose_inner(fs)
    reduce_start(1, 1, reduce_end(1, 0))
    transpose_end(4, copies, None, None)
    reduce_start(1, 2, reduce_end(1, 1))

    def by_lanes(x, np):
        return jnp.where(lane8[:1] < 64, x[2 * np : 2 * np + 1], x[2 * np + 1 : 2 * np + 2])

    def gather_rows(field, np):
        top, bottom = pair(field[every8(2 * np, 64), :], field[every8(2 * np + 1, 64), :])
        return jnp.concatenate([top, bottom], axis=0)

    low = low_half((128, 128))
    for np in range(4):
        at = slice(128 * np, 128 * np + 128)
        more = slice(512 + 128 * np, 512 + 128 * np + 128)
        a0 = by_lanes(alpha0, np)
        x = jnp.where(low, z0[:, 2 * np, :], z0[:, 2 * np + 1, :])
        y = jnp.where(low, q[:, 2 * np, :], q[:, 2 * np + 1, :])
        adjoint[at] = x
        normal[at] = x - a0 * y
        p01[more] = y
        x = gather_rows(fw, np)
        residual[at] = gather_rows(f0, np) - a0 * x
        p23[at] = x
        p23[more] = gather_rows(fs, np)

    sums = reduce_end(1, 2)
    zz1 = column(sums, 0)
    beta = zz1 / zz0
    ww1 = column(sums, 32) + beta * (2.0 * column(sums, 64) + beta * ww0)
    alpha1 = zz1 / ww1
    for np in range(4):
        at = slice(128 * np, 128 * np + 128)
        more = slice(512 + 128 * np, 512 + 128 * np + 128)
        a0, a1, b = (by_lanes(x, np) for x in (alpha0, alpha1, beta))
        x, z1 = adjoint[at], normal[at]
        adjoint[at] = a0 * x + a1 * (z1 + b * x)
        normal[at] = z1 - a1 * (p01[at] + b * p01[more])
        residual[at] = residual[at] - a1 * (p23[more] + b * p23[at])


def turn(*refs):
    for source, out in zip(refs[:3], refs[3:]):
        for np in range(4):
            x = source[128 * np : 128 * np + 128].T
            out[every8(2 * np, 64), :] = x[:64]
            out[every8(2 * np + 1, 64), :] = x[64:]


def shards(
    devices,
    rhs,
    inner_tiles,
    inner_cols,
    send_blocks,
    face_rows,
    face_counts,
    face_tiles,
    contact_send,
    contact_rows,
    contact_pair,
    contact_tiles,
):
    slot = jnp.arange(64, dtype=jnp.int32)
    paired_rows = jnp.sum(
        jnp.where(contact_pair[0][:, None] == slot[None, :], contact_rows[:, None], 0), axis=0
    )
    smem = pl.BlockSpec(memory_space=pltpu.SMEM)
    vmem = pl.BlockSpec(memory_space=pltpu.VMEM)
    copies = sum(size - 1 for size in stage_sizes(devices))
    out = jax.ShapeDtypeStruct((512, 128), F32)
    outs = pl.pallas_call(
        functools.partial(kernel, devices),
        out_shape=[out] * 3,
        in_specs=[smem] * 4 + [vmem] * 7 + [pl.BlockSpec(memory_space=pl.ANY)] * 3,
        out_specs=[vmem] * 3,
        scratch_shapes=[
            pltpu.VMEM(inner_tiles.shape, BF16),
            pltpu.VMEM(face_tiles.shape, BF16),
            pltpu.VMEM(contact_tiles.shape, BF16),
            pltpu.VMEM((64 * PAD, 128), F32),
            pltpu.VMEM((64 * PAD, 128), F32),
            pltpu.VMEM((8192, 256), BF16),
            pltpu.VMEM((32 * PAD, 128), F32),
            pltpu.VMEM((4096, 128), BF16),
            pltpu.VMEM((128, 1024), BF16),
            pltpu.VMEM((128, 256), BF16),
            pltpu.VMEM((128, 256), BF16),
            pltpu.VMEM((128, 256), BF16),
            pltpu.VMEM((1024, 128), F32),
            pltpu.VMEM((1024, 128), F32),
            pltpu.VMEM((128, 512), F32),
            pltpu.VMEM((128, 8, 128), F32),
            pltpu.VMEM((128, 8, 128), F32),
            pltpu.VMEM((512, 128), F32),
            pltpu.VMEM((512, 128), F32),
            pltpu.VMEM((512, 128), F32),
            pltpu.VMEM((128, 8, 128), F32),
            pltpu.VMEM((1024, 128), F32),
            pltpu.VMEM((512, 128), F32),
            pltpu.VMEM((512, 128), F32),
            pltpu.VMEM((APPS, 4, 128, 128), F32),
            pltpu.VMEM((APPS, 4, 128, 128), F32),
            pltpu.VMEM((2, 3, 8, 128), F32),
            pltpu.VMEM((2, copies, 8, 128), F32),
            pltpu.SemaphoreType.DMA((APPS, 3)),
            pltpu.SemaphoreType.DMA((APPS, 3)),
            pltpu.SemaphoreType.DMA((2, 3)),
            pltpu.SemaphoreType.DMA((2, 3)),
            pltpu.SemaphoreType.DMA((3,)),
        ],
        compiler_params=pltpu.CompilerParams(
            collective_id=0, has_side_effects=True, vmem_limit_bytes=56 * 1024 * 1024
        ),
    )(
        inner_cols,
        face_rows,
        paired_rows,
        face_counts,
        rhs.reshape(512, 128),
        inner_cols,
        send_blocks[None],
        contact_send[None],
        face_rows[None],
        paired_rows[None],
        contact_pair,
        inner_tiles,
        face_tiles,
        contact_tiles,
    )
    outs = pl.pallas_call(
        turn, out_shape=[out] * 3, in_specs=[vmem] * 3, out_specs=[vmem] * 3
    )(*outs)
    return tuple(x.reshape(64, 8, 128) for x in outs)


def solution(mesh):
    both = ("dom", "sub")
    field = P(None, None, both)
    devices = 1
    for axis in both:
        devices *= mesh.shape[axis]
    return jax.shard_map(
        functools.partial(shards, devices),
        mesh=mesh,
        in_specs=(
            field,
            P(None, None, None, both),
            P(None, both),
            P(both),
            P(both),
            P(both, None),
            field,
            P(both),
            P(both),
            P(both, None),
            field,
        ),
        out_specs=(field,) * 3,
        check_vma=False,
    )
```

```python
import functools

import jax
import jax.numpy as jnp
from jax import lax
from jax.experimental import pallas as pl
from jax.experimental.pallas import tpu as pltpu
from jax.sharding import PartitionSpec as P

F32 = jnp.float32
BF16 = jnp.bfloat16
APPS = 5
MESH = pl.DeviceIdType.MESH
PAD = 136
NT = (((1,), (1,)), ((), ()))


def stage_sizes(devices):
    bits = devices.bit_length() - 1
    first = min(3, bits - 2)
    second = min(3, bits - first - 1)
    return (1 << first, 1 << second, 1 << (bits - first - second))


def low_half(shape):
    return lax.broadcasted_iota(jnp.int32, shape, 1) < 64


def swap(x):
    return pltpu.roll(x, 64, 1)


def pair(x, y):
    low = low_half(x.shape)
    return jnp.where(low, x, swap(y)), jnp.where(low, swap(x), y)


def split(x):
    high = x.astype(BF16)
    return high, (x - high.astype(F32)).astype(BF16)


def split_wide(x):
    high = x.astype(BF16).astype(F32)
    return high, x - high


def dot(a, b):
    return jnp.dot(a, b, preferred_element_type=F32)


def dot_nt(a, b):
    return lax.dot_general(a, b, NT, preferred_element_type=F32)


def split_dot(product, a, b):
    rows = a.shape[0]
    out = product(jnp.concatenate(split(a), axis=0), b)
    return out[:rows] + out[rows:]


def block8(ref, index):
    return ref[pl.ds(pl.multiple_of(index * 8, 8), 8), :]


def put8(ref, index, value):
    ref[pl.ds(pl.multiple_of(index * 8, 8), 8), :] = value


def every8(first, count):
    return pl.ds(first, count, stride=8)


def kernel(
    devices,
    cols_s,
    frows_s,
    counts_s,
    rhs,
    cols_v,
    send_v,
    csend_v,
    frows_v,
    crows_v,
    pair_v,
    tiles_h,
    ftiles_h,
    ctiles_h,
    adjoint,
    residual,
    normal,
    tiles,
    ftiles,
    ctiles,
    wf0,
    wf1,
    w,
    ef,
    e,
    ohk,
    ohs,
    ohst,
    ohr,
    p01,
    p23,
    zs,
    z0,
    q,
    f0,
    fw,
    fs,
    u,
    xf,
    ps,
    uo,
    sbuf,
    rbuf,
    arsend,
    arrecv,
    xsend,
    xrecv,
    asend,
    arecv,
    fetched,
    crows_w,
    crows_s,
    crows_sem,
):
    fetches = [
        pltpu.make_async_copy(source, target, fetched.at[index])
        for index, (source, target) in enumerate(
            ((ftiles_h, ftiles), (ctiles_h, ctiles), (tiles_h, tiles))
        )
    ]
    for fetch in fetches:
        fetch.start()
    me = lax.axis_index("dom") * 2 + lax.axis_index("sub")
    sizes = stage_sizes(devices)

    def place(index):
        return (index // 2, lax.rem(index, 2))

    lower = lax.rem(me + devices - 1, devices)
    upper = lax.rem(me + 1, devices)
    partner = lax.rem(me + devices // 2, devices)

    def group_peers(stage):
        stride = 1
        for size in sizes[:stage]:
            stride *= size
        size = sizes[stage]
        mine = lax.rem(me // stride, size)
        return [me + (lax.rem(mine + i, size) - mine) * stride for i in range(1, size)]

    peers = [group_peers(stage) for stage in range(3)]
    ar_first = [sum(size - 1 for size in sizes[:stage]) for stage in range(3)]
    everyone = [lower, upper, partner] + peers[0] + peers[1] + peers[2]

    barrier = pltpu.get_barrier_semaphore()
    for other in everyone:
        pl.semaphore_signal(barrier, inc=1, device_id=place(other), device_id_type=MESH)

    row_id = lax.broadcasted_iota(jnp.int32, (128, 128), 0)

    def order_contacts():
        lane_id = lax.broadcasted_iota(jnp.int32, (128, 128), 1)
        matches = jnp.broadcast_to(jnp.concatenate([pair_v[...]] * 2, axis=1), (128, 128)).T == lane_id
        rows = jnp.broadcast_to(jnp.concatenate([crows_v[...]] * 2, axis=1), (128, 128)).T
        rows = jnp.sum(jnp.where(matches & (row_id < 64), rows, 0), axis=0, keepdims=True)
        crows_w[...] = jnp.broadcast_to(rows, (8, 128))
        hand = pltpu.make_async_copy(crows_w, crows_s, crows_sem)
        hand.start()
        hand.wait()

    def prepare_picks():
        for half in range(2):
            for k in range(4):
                at = half * 512 + k * 128
                ohk[:, at : at + 128] = jnp.where(cols_v[k : k + 1, :] == row_id, 1.0, 0.0).astype(BF16)
        picks = jnp.concatenate([send_v[...], csend_v[...]], axis=1) == row_id
        picks = jnp.where(picks, 1.0, 0.0)
        ohs[...] = jnp.concatenate([picks.astype(BF16)] * 2, axis=1)
        picks = picks.T.astype(BF16)
        ohst[...] = jnp.concatenate([picks] * 2, axis=1)
        picks = jnp.concatenate([frows_v[...], crows_w[0:1, :64]], axis=1) == row_id
        picks = jnp.where(picks, 1.0, 0.0).astype(BF16)
        ohr[...] = jnp.concatenate([picks] * 2, axis=1)

    def prepare(a, carry):
        for half, out in ((0, wf0), (1, wf1)):
            x = tiles[2 * half : 2 * half + 2, a].reshape(128, 128)
            x = x.astype(F32).T
            out[pl.ds(a, 64, stride=PAD), :] = x[:64]
            out[pl.ds(64 + a, 64, stride=PAD), :] = x[64:]
        return carry

    def pack(i, carry):
        at = pl.ds(pl.multiple_of(i * 128, 128), 128)
        padded = pl.ds(pl.multiple_of(i * PAD, 8), 128)
        w[at, 0:128] = wf0[padded, :].astype(BF16)
        w[at, 128:256] = wf1[padded, :].astype(BF16)
        return carry

    def prepare_inner():
        fetches[2].wait()
        lax.fori_loop(0, 64, prepare, 0, unroll=8)
        lax.fori_loop(0, 64, pack, 0, unroll=4)

    for n in range(8):
        x = rhs[every8(n, 64), :]
        x = jnp.concatenate([x, x], axis=0).T
        u[:, n, :] = x
        f0[every8(n, 64), :] = jnp.where(low_half((64, 128)), x[:64], x[64:])

    slot = lax.broadcasted_iota(jnp.int32, (64, 64), 0)
    other_slot = lax.broadcasted_iota(jnp.int32, (64, 64), 1)
    side_a = (slot < 32) & (slot < counts_s[0, 0])
    side_b = (slot >= 32) & (slot - 32 < counts_s[0, 1])
    face_pick = jnp.where((slot == other_slot) & (side_a | side_b), 1.0, 0.0)
    contact_pick = jnp.where(pair_v[...] == slot, 1.0, 0.0)
    slot_picks = (face_pick.astype(BF16), contact_pick.astype(BF16))

    def prepare_slots(kind):
        source = (ftiles, ctiles)[kind]

        def turn_four(i, carry):
            parts = []
            for n in range(4):
                parts += [source[4 * i + n]] * 2
            x = dot_nt(slot_picks[kind], jnp.concatenate(parts, axis=0))
            for n in range(4):
                y = x[:, 128 * n : 128 * n + 128]
                for s2 in range(2):
                    at = 32 * s2
                    ef[pl.ds(kind * 16 * PAD + s2 * 64 + 4 * i + n, 16, stride=PAD), :] = jnp.where(
                        low_half((16, 128)), y[at : at + 16], y[at + 16 : at + 32]
                    )
            return carry

        def pack_slots(i, carry):
            at = pl.ds(pl.multiple_of(i * 128, 128), 128)
            e[at, :] = ef[pl.ds(pl.multiple_of(i * PAD, 8), 128), :].astype(BF16)
            return carry

        fetches[kind].wait()
        lax.fori_loop(0, 16, turn_four, 0, unroll=4)
        lax.fori_loop(16 * kind, 16 * kind + 16, pack_slots, 0, unroll=4)

    def tile_at(ref, index):
        return ref[pl.ds(pl.multiple_of(index * 128, 128), 128), :]

    low8 = low_half((8, 128))
    zero8 = jnp.zeros((8, 128), F32)

    def spread(field):
        x = field[...]
        y = swap(x)
        low = low_half(x.shape)
        u[0:64] = jnp.where(low, x, y).reshape(64, 8, 128)
        u[64:128] = jnp.where(low, y, x).reshape(64, 8, 128)


    routes = ((lower, 0, 32, 32), (upper, 32, 64, 0), (partner, 64, 128, 64))

    def exchange(app, kind):
        copies = []
        for index in ((0, 1), (2,))[kind]:
            other, start, stop, to = routes[index]
            copy = pltpu.make_async_remote_copy(
                src_ref=sbuf.at[app, :, pl.ds(start, stop - start), :],
                dst_ref=rbuf.at[app, :, pl.ds(to, stop - start), :],
                send_sem=xsend.at[app, index],
                recv_sem=xrecv.at[app, index],
                device_id=place(other),
                device_id_type=MESH,
            )
            copy.start()
            copies.append(copy)
        return copies

    def reduce_start(which, step, value):
        stage = (1, 0, 2)[step]
        arsend[which, stage] = value
        for index, other in enumerate(peers[stage]):
            pltpu.make_async_remote_copy(
                src_ref=arsend.at[which, stage],
                dst_ref=arrecv.at[which, ar_first[stage] + index],
                send_sem=asend.at[which, stage],
                recv_sem=arecv.at[which, stage],
                device_id=place(other),
                device_id_type=MESH,
            ).start()

    def reduce_end(which, step):
        stage = (1, 0, 2)[step]
        arrived = arrecv.at[which, pl.ds(ar_first[stage], len(peers[stage]))]
        pltpu.make_async_copy(arrived, arrived, arecv.at[which, stage]).wait()
        pltpu.make_async_copy(arrived, arrived, asend.at[which, stage]).wait()
        total = arsend[which, stage]
        for index in range(len(peers[stage])):
            total = total + arrecv[which, ar_first[stage] + index]
        return total

    def transpose_slots(app):
        copies = []
        if app == 0:
            prepare_slots(0)
        for kind, rows in enumerate((lambda i: frows_s[i], lambda i: crows_s[0, i])):

            def body(tp, carry):
                parts = []
                for h in range(2):
                    parts.append(jnp.where(low8, u[rows(16 * h + tp)], zero8))
                    parts.append(jnp.where(low8, zero8, u[rows(32 + 16 * h + tp)]))
                out = split_dot(dot, jnp.concatenate(parts, axis=0), tile_at(e, 16 * kind + tp))
                put8(ps, 32 * kind + tp, jnp.where(low8, out[0:8], out[16:24]))
                put8(ps, 32 * kind + 16 + tp, jnp.where(low8, out[8:16], out[24:32]))
                return carry

            lax.fori_loop(0, 16, body, 0, unroll=16)
            for np in range(4):
                at = 256 * kind + 2 * np
                x, y = pair(ps[every8(at, 32), :], ps[every8(at + 1, 32), :])
                sbuf[app, np, 64 * kind : 64 * kind + 64] = jnp.concatenate(
                    [x[:16], y[:16], x[16:], y[16:]], axis=0
                )
            if app == 0 and kind == 0:
                pl.semaphore_wait(barrier, len(everyone))
            copies += exchange(app, kind)
            if app == 0 and kind == 0:
                order_contacts()
                prepare_slots(1)
        return copies

    def transpose_inner(field):
        def body(jp, carry):
            high, rest = split_wide(block8(field, jp))
            parts = [
                jnp.where(low8, high, zero8),
                jnp.where(low8, rest, zero8),
                jnp.where(low8, zero8, high),
                jnp.where(low8, zero8, rest),
            ]
            out = dot(jnp.concatenate(parts, axis=0).astype(BF16), tile_at(w, jp))
            x = out[0:8] + out[8:16]
            y = out[16:24] + out[24:32]
            put8(p01, jp, x[:, :128])
            put8(p23, jp, x[:, 128:])
            put8(p01, 64 + jp, y[:, :128])
            put8(p23, 64 + jp, y[:, 128:])
            return carry

        lax.fori_loop(0, 64, body, 0, unroll=16)

    def put_turned(out, first, np, x):
        x = x.T
        out[every8(first + 2 * np, 64), :] = x[:64]
        out[every8(first + 2 * np + 1, 64), :] = x[64:]

    def halves(parts):
        x = jnp.concatenate(parts, axis=1)
        return jnp.concatenate(split(x), axis=0)

    def transpose_end(app, copies, result, send_app):
        parts = []
        for np in range(4):
            k0, k1 = pair(p01[every8(2 * np, 128), :], p01[every8(2 * np + 1, 128), :])
            k2, k3 = pair(p23[every8(2 * np, 128), :], p23[every8(2 * np + 1, 128), :])
            parts.append(jnp.concatenate([k0, k1, k2, k3], axis=0))
        zs[...] = dot(ohk[...], halves(parts))
        for copy in copies:
            copy.wait()
        low = low_half((128, 128))
        z = zs[...] + dot(ohs[...], halves([rbuf[app, np] for np in range(4)]))
        if send_app is not None:
            terms = jnp.concatenate(split(z), axis=0)
            copies = []
            for kind in range(2):
                at = slice(64 * kind, 64 * kind + 64)
                x = dot(ohst[at], terms)
                for np in range(4):
                    sbuf[send_app, np, at] = x[:, 128 * np : 128 * np + 128]
                copies += exchange(send_app, kind)
        for np in range(4):
            x = z[:, 128 * np : 128 * np + 128]
            if result is None:
                put_turned(p01, 0, np, x)
            else:
                other = swap(x)
                result[:, 2 * np, :] = jnp.where(low, x, other)
                result[:, 2 * np + 1, :] = jnp.where(low, other, x)
        return copies

    def forward_inner(field, result):
        def body(jp, carry):
            parts = []
            for j2 in range(2):
                j = j2 * 64 + jp
                v = [field[cols_s[k, j]] for k in range(4)]
                x = jnp.concatenate(
                    [jnp.where(low8, v[0], v[1]), jnp.where(low8, v[2], v[3])], axis=1
                )
                parts += list(split_wide(x))
            out = dot_nt(jnp.concatenate(parts, axis=0).astype(BF16), tile_at(w, jp))
            put8(result, jp, jnp.where(low8, out[0:8] + out[8:16], out[16:24] + out[24:32]))
            return carry

        lax.fori_loop(0, 64, body, 0, unroll=16)

    def forward_end(app, copies, result):
        low = low_half((64, 128))
        first = lax.rem(lax.broadcasted_iota(jnp.int32, (64, 128), 0) // 16, 2) == 0
        mine = low == first
        for kind in (1, 0):
            for copy in (copies[:2], copies[2:])[kind]:
                copy.wait()
            for np in range(4):
                x = rbuf[app, np, 64 * kind : 64 * kind + 64]
                y = swap(x)
                at = 512 * kind + 2 * np
                xf[every8(at, 64), :] = jnp.where(mine, jnp.where(first, x, y), 0.0)
                xf[every8(at + 1, 64), :] = jnp.where(mine, jnp.where(first, y, x), 0.0)

            def body(tp, carry):
                parts = []
                for h in range(2):
                    for s2 in range(2):
                        parts.append(block8(xf, 64 * kind + 32 * s2 + 16 * h + tp))
                tile = tile_at(e, 16 * kind + tp)
                out = split_dot(dot_nt, jnp.concatenate(parts, axis=0), tile)
                put8(uo, 32 * kind + tp, jnp.where(low8, out[0:8], out[8:16]))
                put8(uo, 32 * kind + 16 + tp, jnp.where(low8, out[16:24], out[24:32]))
                return carry

            lax.fori_loop(0, 16, body, 0, unroll=16)
        parts = []
        for np in range(4):
            s0, s1 = pair(uo[every8(2 * np, 64), :], uo[every8(2 * np + 1, 64), :])
            parts.append(jnp.concatenate([s0[:32], s1[:32], s0[32:], s1[32:]], axis=0))
        y = dot(ohr[...], halves(parts))
        sums = []
        for np in range(4):
            x = y[:, 128 * np : 128 * np + 128]
            for n, x in enumerate(pair(x[:64], x[64:])):
                sums.append(result[every8(2 * np + n, 64), :] + x)
        for n, x in enumerate(sums):
            result[every8(n, 64), :] = x

    def total(x):
        x = jnp.sum(x.reshape(-1, 8, 128), axis=0)
        return jnp.broadcast_to(jnp.sum(x, axis=1, keepdims=True), (8, 128))

    lane8 = lax.broadcasted_iota(jnp.int32, (8, 128), 1)

    def column(x, index):
        return jnp.broadcast_to(x[:, index : index + 1], (8, 128))

    def each(x, rows):
        return jnp.broadcast_to(x[None], (rows // 8, 8, 128)).reshape(rows, 128)

    copies = transpose_slots(0)
    prepare_picks()
    prepare_inner()
    transpose_inner(f0)
    copies = transpose_end(0, copies, z0, 1)
    forward_inner(z0, fw)
    zz = total(z0[...] * z0[...]) * 0.5
    forward_end(1, copies, fw)
    ww = total(fw[...] * fw[...])
    reduce_start(0, 0, jnp.where(lane8 < 64, zz, ww))
    spread(fw)
    copies = transpose_slots(2)
    transpose_inner(fw)
    reduce_start(0, 1, reduce_end(0, 0))
    copies = transpose_end(2, copies, q, 3)
    forward_inner(q, fs)
    reduce_start(0, 2, reduce_end(0, 1))
    forward_end(3, copies, fs)
    sums = reduce_end(0, 2)
    zz0 = column(sums, 0)
    ww0 = column(sums, 64)
    alpha0 = zz0 / ww0
    s1 = fw[...] - each(alpha0, 512) * fs[...]
    fs[...] = s1
    z1 = z0[...] - alpha0[None] * q[...]
    zz = total(z1 * z1) * 0.5
    ss = total(s1 * s1)
    sw = total(s1 * fw[...])
    reduce_start(1, 0, jnp.where(lane8 < 32, zz, jnp.where(lane8 < 64, ss, sw)))
    spread(fs)
    copies = transpose_slots(4)
    transpose_inner(fs)
    reduce_start(1, 1, reduce_end(1, 0))
    transpose_end(4, copies, None, None)
    reduce_start(1, 2, reduce_end(1, 1))

    def gather_rows(field, np):
        top, bottom = pair(field[every8(2 * np, 64), :], field[every8(2 * np + 1, 64), :])
        return jnp.concatenate([top, bottom], axis=0)

    low = low_half((128, 128))
    for np in range(4):
        for source, out, first in ((z0, adjoint, 0), (q, p01, 512)):
            x = jnp.where(low, source[:, 2 * np, :], source[:, 2 * np + 1, :])
            put_turned(out, first, np, x)
        for source, out, first in ((f0, residual, 0), (fw, p23, 0), (fs, p23, 512)):
            put_turned(out, first, np, gather_rows(source, np))
    a0 = each(alpha0, 512)
    normal[...] = adjoint[...] - a0 * p01[512:1024]
    residual[...] = residual[...] - a0 * p23[0:512]

    sums = reduce_end(1, 2)
    zz1 = column(sums, 0)
    beta = zz1 / zz0
    ww1 = column(sums, 32) + beta * (2.0 * column(sums, 64) + beta * ww0)
    alpha1 = zz1 / ww1
    a1, b = each(alpha1, 512), each(beta, 512)
    x, z1 = adjoint[...], normal[...]
    adjoint[...] = a0 * x + a1 * (z1 + b * x)
    normal[...] = z1 - a1 * (p01[0:512] + b * p01[512:1024])
    residual[...] = residual[...] - a1 * (p23[512:1024] + b * p23[0:512])


def hand_over(*refs):
    for source, out in zip(refs[:3], refs[3:]):
        out[...] = source[...]


def shards(
    devices,
    rhs,
    inner_tiles,
    inner_cols,
    send_blocks,
    face_rows,
    face_counts,
    face_tiles,
    contact_send,
    contact_rows,
    contact_pair,
    contact_tiles,
):
    smem = pl.BlockSpec(memory_space=pltpu.SMEM)
    vmem = pl.BlockSpec(memory_space=pltpu.VMEM)
    copies = sum(size - 1 for size in stage_sizes(devices))
    out = jax.ShapeDtypeStruct((512, 128), F32)
    outs = pl.pallas_call(
        functools.partial(kernel, devices),
        out_shape=[out] * 3,
        in_specs=[smem] * 3 + [vmem] * 7 + [pl.BlockSpec(memory_space=pl.ANY)] * 3,
        out_specs=[vmem] * 3,
        scratch_shapes=[
            pltpu.VMEM(inner_tiles.shape, BF16),
            pltpu.VMEM(face_tiles.shape, BF16),
            pltpu.VMEM(contact_tiles.shape, BF16),
            pltpu.VMEM((64 * PAD, 128), F32),
            pltpu.VMEM((64 * PAD, 128), F32),
            pltpu.VMEM((8192, 256), BF16),
            pltpu.VMEM((32 * PAD, 128), F32),
            pltpu.VMEM((4096, 128), BF16),
            pltpu.VMEM((128, 1024), BF16),
            pltpu.VMEM((128, 256), BF16),
            pltpu.VMEM((128, 256), BF16),
            pltpu.VMEM((128, 256), BF16),
            pltpu.VMEM((1024, 128), F32),
            pltpu.VMEM((1024, 128), F32),
            pltpu.VMEM((128, 512), F32),
            pltpu.VMEM((128, 8, 128), F32),
            pltpu.VMEM((128, 8, 128), F32),
            pltpu.VMEM((512, 128), F32),
            pltpu.VMEM((512, 128), F32),
            pltpu.VMEM((512, 128), F32),
            pltpu.VMEM((128, 8, 128), F32),
            pltpu.VMEM((1024, 128), F32),
            pltpu.VMEM((512, 128), F32),
            pltpu.VMEM((512, 128), F32),
            pltpu.VMEM((APPS, 4, 128, 128), F32),
            pltpu.VMEM((APPS, 4, 128, 128), F32),
            pltpu.VMEM((2, 3, 8, 128), F32),
            pltpu.VMEM((2, copies, 8, 128), F32),
            pltpu.SemaphoreType.DMA((APPS, 3)),
            pltpu.SemaphoreType.DMA((APPS, 3)),
            pltpu.SemaphoreType.DMA((2, 3)),
            pltpu.SemaphoreType.DMA((2, 3)),
            pltpu.SemaphoreType.DMA((3,)),
            pltpu.VMEM((8, 128), jnp.int32),
            pltpu.SMEM((8, 128), jnp.int32),
            pltpu.SemaphoreType.DMA,
        ],
        compiler_params=pltpu.CompilerParams(
            collective_id=0, has_side_effects=True, vmem_limit_bytes=56 * 1024 * 1024
        ),
    )(
        inner_cols,
        face_rows,
        face_counts,
        rhs.reshape(512, 128),
        inner_cols,
        send_blocks[None],
        contact_send[None],
        face_rows[None],
        contact_rows[None],
        contact_pair,
        inner_tiles,
        face_tiles,
        contact_tiles,
    )
    outs = pl.pallas_call(
        hand_over, out_shape=[out] * 3, in_specs=[vmem] * 3, out_specs=[vmem] * 3
    )(*outs)
    return tuple(x.reshape(64, 8, 128) for x in outs)


def solution(mesh):
    both = ("dom", "sub")
    field = P(None, None, both)
    devices = 1
    for axis in both:
        devices *= mesh.shape[axis]
    return jax.shard_map(
        functools.partial(shards, devices),
        mesh=mesh,
        in_specs=(
            field,
            P(None, None, None, both),
            P(None, both),
            P(both),
            P(both),
            P(both, None),
            field,
            P(both),
            P(both),
            P(both, None),
            field,
        ),
        out_specs=(field,) * 3,
        check_vma=False,
    )
```

```python
import functools

import jax
import jax.numpy as jnp
from jax import lax
from jax.experimental import pallas as pl
from jax.experimental.pallas import tpu as pltpu
from jax.sharding import PartitionSpec as P

F32 = jnp.float32
BF16 = jnp.bfloat16
APPS = 5
MESH = pl.DeviceIdType.MESH
PAD = 136
NT = (((1,), (1,)), ((), ()))


def stage_sizes(devices):
    bits = devices.bit_length() - 1
    first = min(3, bits - 2)
    second = min(3, bits - first - 1)
    return (1 << first, 1 << second, 1 << (bits - first - second))


def low_half(shape):
    return lax.broadcasted_iota(jnp.int32, shape, 1) < 64


def swap(x):
    return pltpu.roll(x, 64, 1)


def pair(x, y):
    low = low_half(x.shape)
    return jnp.where(low, x, swap(y)), jnp.where(low, swap(x), y)


def split(x):
    high = x.astype(BF16)
    return high, (x - high.astype(F32)).astype(BF16)


def split_wide(x):
    high = x.astype(BF16).astype(F32)
    return high, x - high


def dot(a, b):
    return jnp.dot(a, b, preferred_element_type=F32)


def dot_nt(a, b):
    return lax.dot_general(a, b, NT, preferred_element_type=F32)


def split_dot(product, a, b):
    rows = a.shape[0]
    out = product(jnp.concatenate(split(a), axis=0), b)
    return out[:rows] + out[rows:]


def block8(ref, index):
    return ref[pl.ds(pl.multiple_of(index * 8, 8), 8), :]


def put8(ref, index, value):
    ref[pl.ds(pl.multiple_of(index * 8, 8), 8), :] = value


def every8(first, count):
    return pl.ds(first, count, stride=8)


def kernel(
    devices,
    cols_s,
    frows_s,
    counts_s,
    rhs,
    cols_v,
    send_v,
    csend_v,
    frows_v,
    crows_v,
    pair_v,
    tiles_h,
    ftiles_h,
    ctiles_h,
    adjoint,
    residual,
    normal,
    tiles,
    ftiles,
    ctiles,
    wf0,
    wf1,
    w,
    ef,
    e,
    ohk,
    ohs,
    ohst,
    ohr,
    p01,
    p23,
    zs,
    z0,
    q,
    f0,
    fw,
    fs,
    u,
    xf,
    ps,
    uo,
    sbuf,
    rbuf,
    arsend,
    arrecv,
    xsend,
    xrecv,
    asend,
    arecv,
    fetched,
    crows_w,
    crows_s,
    crows_sem,
):
    fetches = [
        pltpu.make_async_copy(source, target, fetched.at[index])
        for index, (source, target) in enumerate(
            ((ftiles_h, ftiles), (ctiles_h, ctiles), (tiles_h, tiles))
        )
    ]
    for fetch in fetches:
        fetch.start()
    me = lax.axis_index("dom") * 2 + lax.axis_index("sub")
    sizes = stage_sizes(devices)

    def place(index):
        return (index // 2, lax.rem(index, 2))

    lower = lax.rem(me + devices - 1, devices)
    upper = lax.rem(me + 1, devices)
    partner = lax.rem(me + devices // 2, devices)

    def group_peers(stage):
        stride = 1
        for size in sizes[:stage]:
            stride *= size
        size = sizes[stage]
        mine = lax.rem(me // stride, size)
        return [me + (lax.rem(mine + i, size) - mine) * stride for i in range(1, size)]

    peers = [group_peers(stage) for stage in range(3)]
    ar_first = [sum(size - 1 for size in sizes[:stage]) for stage in range(3)]
    everyone = [lower, upper, partner] + peers[0] + peers[1] + peers[2]

    barrier = pltpu.get_barrier_semaphore()
    for other in everyone:
        pl.semaphore_signal(barrier, inc=1, device_id=place(other), device_id_type=MESH)

    row_id = lax.broadcasted_iota(jnp.int32, (128, 128), 0)
    for half in range(2):
        for k in range(4):
            at = half * 512 + k * 128
            ohk[:, at : at + 128] = jnp.where(cols_v[k : k + 1, :] == row_id, 1.0, 0.0).astype(BF16)
    picks = jnp.concatenate([send_v[...], csend_v[...]], axis=1) == row_id
    picks = jnp.where(picks, 1.0, 0.0)
    ohs[...] = jnp.concatenate([picks.astype(BF16)] * 2, axis=1)
    picks = picks.T.astype(BF16)
    ohst[...] = jnp.concatenate([picks] * 2, axis=1)
    lane_id = lax.broadcasted_iota(jnp.int32, (128, 128), 1)
    matches = jnp.broadcast_to(jnp.concatenate([pair_v[...]] * 2, axis=1), (128, 128)).T == lane_id
    rows = jnp.broadcast_to(jnp.concatenate([crows_v[...]] * 2, axis=1), (128, 128)).T
    rows = jnp.sum(jnp.where(matches & (row_id < 64), rows, 0), axis=0, keepdims=True)
    crows_w[...] = jnp.broadcast_to(rows, (8, 128))
    hand = pltpu.make_async_copy(crows_w, crows_s, crows_sem)
    hand.start()
    hand.wait()
    picks = jnp.concatenate([frows_v[...], rows[:, :64]], axis=1) == row_id
    picks = jnp.where(picks, 1.0, 0.0).astype(BF16)
    ohr[...] = jnp.concatenate([picks] * 2, axis=1)

    def prepare(a, carry):
        for half, out in ((0, wf0), (1, wf1)):
            x = tiles[2 * half : 2 * half + 2, a].reshape(128, 128)
            x = x.astype(F32).T
            out[pl.ds(a, 64, stride=PAD), :] = x[:64]
            out[pl.ds(64 + a, 64, stride=PAD), :] = x[64:]
        return carry

    def pack(i, carry):
        at = pl.ds(pl.multiple_of(i * 128, 128), 128)
        padded = pl.ds(pl.multiple_of(i * PAD, 8), 128)
        w[at, 0:128] = wf0[padded, :].astype(BF16)
        w[at, 128:256] = wf1[padded, :].astype(BF16)
        return carry

    def prepare_inner():
        fetches[2].wait()
        lax.fori_loop(0, 64, prepare, 0, unroll=8)
        lax.fori_loop(0, 64, pack, 0, unroll=4)

    for n in range(8):
        x = rhs[every8(n, 64), :]
        x = jnp.concatenate([x, x], axis=0).T
        u[:, n, :] = x
        f0[every8(n, 64), :] = jnp.where(low_half((64, 128)), x[:64], x[64:])

    slot = lax.broadcasted_iota(jnp.int32, (64, 64), 0)
    other_slot = lax.broadcasted_iota(jnp.int32, (64, 64), 1)
    side_a = (slot < 32) & (slot < counts_s[0, 0])
    side_b = (slot >= 32) & (slot - 32 < counts_s[0, 1])
    face_pick = jnp.where((slot == other_slot) & (side_a | side_b), 1.0, 0.0)
    contact_pick = jnp.where(pair_v[...] == slot, 1.0, 0.0)
    slot_picks = (face_pick.astype(BF16), contact_pick.astype(BF16))

    def prepare_slots(i, carry):
        for kind, source in enumerate((ftiles, ctiles)):
            parts = []
            for n in range(4):
                parts += [source[4 * i + n]] * 2
            x = dot_nt(slot_picks[kind], jnp.concatenate(parts, axis=0))
            for n in range(4):
                y = x[:, 128 * n : 128 * n + 128]
                for s2 in range(2):
                    at = 32 * s2
                    ef[pl.ds(kind * 16 * PAD + s2 * 64 + 4 * i + n, 16, stride=PAD), :] = jnp.where(
                        low_half((16, 128)), y[at : at + 16], y[at + 16 : at + 32]
                    )
        return carry

    for fetch in fetches[:2]:
        fetch.wait()
    lax.fori_loop(0, 16, prepare_slots, 0, unroll=2)

    def pack_slots(i, carry):
        at = pl.ds(pl.multiple_of(i * 128, 128), 128)
        e[at, :] = ef[pl.ds(pl.multiple_of(i * PAD, 8), 128), :].astype(BF16)
        return carry

    lax.fori_loop(0, 32, pack_slots, 0, unroll=4)

    def tile_at(ref, index):
        return ref[pl.ds(pl.multiple_of(index * 128, 128), 128), :]

    low8 = low_half((8, 128))
    zero8 = jnp.zeros((8, 128), F32)

    def spread(field):
        x = field[...]
        y = swap(x)
        low = low_half(x.shape)
        u[0:64] = jnp.where(low, x, y).reshape(64, 8, 128)
        u[64:128] = jnp.where(low, y, x).reshape(64, 8, 128)


    routes = ((lower, 0, 32, 32), (upper, 32, 64, 0), (partner, 64, 128, 64))

    def exchange(app, kind):
        copies = []
        for index in ((0, 1), (2,))[kind]:
            other, start, stop, to = routes[index]
            copy = pltpu.make_async_remote_copy(
                src_ref=sbuf.at[app, :, pl.ds(start, stop - start), :],
                dst_ref=rbuf.at[app, :, pl.ds(to, stop - start), :],
                send_sem=xsend.at[app, index],
                recv_sem=xrecv.at[app, index],
                device_id=place(other),
                device_id_type=MESH,
            )
            copy.start()
            copies.append(copy)
        return copies

    def reduce_start(which, step, value):
        stage = (1, 0, 2)[step]
        arsend[which, stage] = value
        for index, other in enumerate(peers[stage]):
            pltpu.make_async_remote_copy(
                src_ref=arsend.at[which, stage],
                dst_ref=arrecv.at[which, ar_first[stage] + index],
                send_sem=asend.at[which, stage],
                recv_sem=arecv.at[which, stage],
                device_id=place(other),
                device_id_type=MESH,
            ).start()

    def reduce_end(which, step):
        stage = (1, 0, 2)[step]
        arrived = arrecv.at[which, pl.ds(ar_first[stage], len(peers[stage]))]
        pltpu.make_async_copy(arrived, arrived, arecv.at[which, stage]).wait()
        pltpu.make_async_copy(arrived, arrived, asend.at[which, stage]).wait()
        total = arsend[which, stage]
        for index in range(len(peers[stage])):
            total = total + arrecv[which, ar_first[stage] + index]
        return total

    def transpose_slots(app):
        copies = []
        for kind, rows in enumerate((lambda i: frows_s[i], lambda i: crows_s[0, i])):

            def body(tp, carry):
                parts = []
                for h in range(2):
                    parts.append(jnp.where(low8, u[rows(16 * h + tp)], zero8))
                    parts.append(jnp.where(low8, zero8, u[rows(32 + 16 * h + tp)]))
                out = split_dot(dot, jnp.concatenate(parts, axis=0), tile_at(e, 16 * kind + tp))
                put8(ps, 32 * kind + tp, jnp.where(low8, out[0:8], out[16:24]))
                put8(ps, 32 * kind + 16 + tp, jnp.where(low8, out[8:16], out[24:32]))
                return carry

            lax.fori_loop(0, 16, body, 0, unroll=16)
            for np in range(4):
                at = 256 * kind + 2 * np
                x, y = pair(ps[every8(at, 32), :], ps[every8(at + 1, 32), :])
                sbuf[app, np, 64 * kind : 64 * kind + 64] = jnp.concatenate(
                    [x[:16], y[:16], x[16:], y[16:]], axis=0
                )
            if app == 0 and kind == 0:
                pl.semaphore_wait(barrier, len(everyone))
            copies += exchange(app, kind)
        return copies

    def transpose_inner(field):
        def body(jp, carry):
            high, rest = split_wide(block8(field, jp))
            parts = [
                jnp.where(low8, high, zero8),
                jnp.where(low8, rest, zero8),
                jnp.where(low8, zero8, high),
                jnp.where(low8, zero8, rest),
            ]
            out = dot(jnp.concatenate(parts, axis=0).astype(BF16), tile_at(w, jp))
            x = out[0:8] + out[8:16]
            y = out[16:24] + out[24:32]
            put8(p01, jp, x[:, :128])
            put8(p23, jp, x[:, 128:])
            put8(p01, 64 + jp, y[:, :128])
            put8(p23, 64 + jp, y[:, 128:])
            return carry

        lax.fori_loop(0, 64, body, 0, unroll=16)

    def put_turned(out, first, np, x):
        x = x.T
        out[every8(first + 2 * np, 64), :] = x[:64]
        out[every8(first + 2 * np + 1, 64), :] = x[64:]

    def halves(parts):
        x = jnp.concatenate(parts, axis=1)
        return jnp.concatenate(split(x), axis=0)

    def transpose_end(app, copies, result, send_app):
        parts = []
        for np in range(4):
            k0, k1 = pair(p01[every8(2 * np, 128), :], p01[every8(2 * np + 1, 128), :])
            k2, k3 = pair(p23[every8(2 * np, 128), :], p23[every8(2 * np + 1, 128), :])
            parts.append(jnp.concatenate([k0, k1, k2, k3], axis=0))
        zs[...] = dot(ohk[...], halves(parts))
        for copy in copies:
            copy.wait()
        low = low_half((128, 128))
        z = zs[...] + dot(ohs[...], halves([rbuf[app, np] for np in range(4)]))
        if send_app is not None:
            x = dot(ohst[...], jnp.concatenate(split(z), axis=0))
            for np in range(4):
                sbuf[send_app, np] = x[:, 128 * np : 128 * np + 128]
            copies = exchange(send_app, 0) + exchange(send_app, 1)
        for np in range(4):
            x = z[:, 128 * np : 128 * np + 128]
            if result is None:
                put_turned(p01, 0, np, x)
            else:
                other = swap(x)
                result[:, 2 * np, :] = jnp.where(low, x, other)
                result[:, 2 * np + 1, :] = jnp.where(low, other, x)
        return copies

    def forward_inner(field, result):
        def body(jp, carry):
            parts = []
            for j2 in range(2):
                j = j2 * 64 + jp
                v = [field[cols_s[k, j]] for k in range(4)]
                x = jnp.concatenate(
                    [jnp.where(low8, v[0], v[1]), jnp.where(low8, v[2], v[3])], axis=1
                )
                parts += list(split_wide(x))
            out = dot_nt(jnp.concatenate(parts, axis=0).astype(BF16), tile_at(w, jp))
            put8(result, jp, jnp.where(low8, out[0:8] + out[8:16], out[16:24] + out[24:32]))
            return carry

        lax.fori_loop(0, 64, body, 0, unroll=16)

    def forward_end(app, copies, result):
        low = low_half((64, 128))
        first = lax.rem(lax.broadcasted_iota(jnp.int32, (64, 128), 0) // 16, 2) == 0
        mine = low == first
        for kind in (1, 0):
            for copy in (copies[:2], copies[2:])[kind]:
                copy.wait()
            for np in range(4):
                x = rbuf[app, np, 64 * kind : 64 * kind + 64]
                y = swap(x)
                at = 512 * kind + 2 * np
                xf[every8(at, 64), :] = jnp.where(mine, jnp.where(first, x, y), 0.0)
                xf[every8(at + 1, 64), :] = jnp.where(mine, jnp.where(first, y, x), 0.0)

            def body(tp, carry):
                parts = []
                for h in range(2):
                    for s2 in range(2):
                        parts.append(block8(xf, 64 * kind + 32 * s2 + 16 * h + tp))
                tile = tile_at(e, 16 * kind + tp)
                out = split_dot(dot_nt, jnp.concatenate(parts, axis=0), tile)
                put8(uo, 32 * kind + tp, jnp.where(low8, out[0:8], out[8:16]))
                put8(uo, 32 * kind + 16 + tp, jnp.where(low8, out[16:24], out[24:32]))
                return carry

            lax.fori_loop(0, 16, body, 0, unroll=16)
        parts = []
        for np in range(4):
            s0, s1 = pair(uo[every8(2 * np, 64), :], uo[every8(2 * np + 1, 64), :])
            parts.append(jnp.concatenate([s0[:32], s1[:32], s0[32:], s1[32:]], axis=0))
        y = dot(ohr[...], halves(parts))
        sums = []
        for np in range(4):
            x = y[:, 128 * np : 128 * np + 128]
            for n, x in enumerate(pair(x[:64], x[64:])):
                sums.append(result[every8(2 * np + n, 64), :] + x)
        for n, x in enumerate(sums):
            result[every8(n, 64), :] = x

    def total(x):
        x = jnp.sum(x.reshape(-1, 8, 128), axis=0)
        return jnp.broadcast_to(jnp.sum(x, axis=1, keepdims=True), (8, 128))

    lane8 = lax.broadcasted_iota(jnp.int32, (8, 128), 1)

    def column(x, index):
        return jnp.broadcast_to(x[:, index : index + 1], (8, 128))

    def each(x, rows):
        return jnp.broadcast_to(x[None], (rows // 8, 8, 128)).reshape(rows, 128)

    copies = transpose_slots(0)
    prepare_inner()
    transpose_inner(f0)
    copies = transpose_end(0, copies, z0, 1)
    forward_inner(z0, fw)
    zz = total(z0[...] * z0[...]) * 0.5
    forward_end(1, copies, fw)
    ww = total(fw[...] * fw[...])
    reduce_start(0, 0, jnp.where(lane8 < 64, zz, ww))
    spread(fw)
    copies = transpose_slots(2)
    transpose_inner(fw)
    reduce_start(0, 1, reduce_end(0, 0))
    copies = transpose_end(2, copies, q, 3)
    forward_inner(q, fs)
    reduce_start(0, 2, reduce_end(0, 1))
    forward_end(3, copies, fs)
    sums = reduce_end(0, 2)
    zz0 = column(sums, 0)
    ww0 = column(sums, 64)
    alpha0 = zz0 / ww0
    s1 = fw[...] - each(alpha0, 512) * fs[...]
    fs[...] = s1
    z1 = z0[...] - alpha0[None] * q[...]
    zz = total(z1 * z1) * 0.5
    ss = total(s1 * s1)
    sw = total(s1 * fw[...])
    reduce_start(1, 0, jnp.where(lane8 < 32, zz, jnp.where(lane8 < 64, ss, sw)))
    spread(fs)
    copies = transpose_slots(4)
    transpose_inner(fs)
    reduce_start(1, 1, reduce_end(1, 0))
    transpose_end(4, copies, None, None)
    reduce_start(1, 2, reduce_end(1, 1))

    def gather_rows(field, np):
        top, bottom = pair(field[every8(2 * np, 64), :], field[every8(2 * np + 1, 64), :])
        return jnp.concatenate([top, bottom], axis=0)

    low = low_half((128, 128))
    for np in range(4):
        for source, out, first in ((z0, adjoint, 0), (q, p01, 512)):
            x = jnp.where(low, source[:, 2 * np, :], source[:, 2 * np + 1, :])
            put_turned(out, first, np, x)
        for source, out, first in ((f0, residual, 0), (fw, p23, 0), (fs, p23, 512)):
            put_turned(out, first, np, gather_rows(source, np))
    a0 = each(alpha0, 512)
    normal[...] = adjoint[...] - a0 * p01[512:1024]
    residual[...] = residual[...] - a0 * p23[0:512]

    sums = reduce_end(1, 2)
    zz1 = column(sums, 0)
    beta = zz1 / zz0
    ww1 = column(sums, 32) + beta * (2.0 * column(sums, 64) + beta * ww0)
    alpha1 = zz1 / ww1
    a1, b = each(alpha1, 512), each(beta, 512)
    x, z1 = adjoint[...], normal[...]
    adjoint[...] = a0 * x + a1 * (z1 + b * x)
    normal[...] = z1 - a1 * (p01[0:512] + b * p01[512:1024])
    residual[...] = residual[...] - a1 * (p23[512:1024] + b * p23[0:512])


def hand_over(*refs):
    for source, out in zip(refs[:3], refs[3:]):
        out[...] = source[...]


def shards(
    devices,
    rhs,
    inner_tiles,
    inner_cols,
    send_blocks,
    face_rows,
    face_counts,
    face_tiles,
    contact_send,
    contact_rows,
    contact_pair,
    contact_tiles,
):
    smem = pl.BlockSpec(memory_space=pltpu.SMEM)
    vmem = pl.BlockSpec(memory_space=pltpu.VMEM)
    copies = sum(size - 1 for size in stage_sizes(devices))
    out = jax.ShapeDtypeStruct((512, 128), F32)
    outs = pl.pallas_call(
        functools.partial(kernel, devices),
        out_shape=[out] * 3,
        in_specs=[smem] * 3 + [vmem] * 7 + [pl.BlockSpec(memory_space=pl.ANY)] * 3,
        out_specs=[vmem] * 3,
        scratch_shapes=[
            pltpu.VMEM(inner_tiles.shape, BF16),
            pltpu.VMEM(face_tiles.shape, BF16),
            pltpu.VMEM(contact_tiles.shape, BF16),
            pltpu.VMEM((64 * PAD, 128), F32),
            pltpu.VMEM((64 * PAD, 128), F32),
            pltpu.VMEM((8192, 256), BF16),
            pltpu.VMEM((32 * PAD, 128), F32),
            pltpu.VMEM((4096, 128), BF16),
            pltpu.VMEM((128, 1024), BF16),
            pltpu.VMEM((128, 256), BF16),
            pltpu.VMEM((128, 256), BF16),
            pltpu.VMEM((128, 256), BF16),
            pltpu.VMEM((1024, 128), F32),
            pltpu.VMEM((1024, 128), F32),
            pltpu.VMEM((128, 512), F32),
            pltpu.VMEM((128, 8, 128), F32),
            pltpu.VMEM((128, 8, 128), F32),
            pltpu.VMEM((512, 128), F32),
            pltpu.VMEM((512, 128), F32),
            pltpu.VMEM((512, 128), F32),
            pltpu.VMEM((128, 8, 128), F32),
            pltpu.VMEM((1024, 128), F32),
            pltpu.VMEM((512, 128), F32),
            pltpu.VMEM((512, 128), F32),
            pltpu.VMEM((APPS, 4, 128, 128), F32),
            pltpu.VMEM((APPS, 4, 128, 128), F32),
            pltpu.VMEM((2, 3, 8, 128), F32),
            pltpu.VMEM((2, copies, 8, 128), F32),
            pltpu.SemaphoreType.DMA((APPS, 3)),
            pltpu.SemaphoreType.DMA((APPS, 3)),
            pltpu.SemaphoreType.DMA((2, 3)),
            pltpu.SemaphoreType.DMA((2, 3)),
            pltpu.SemaphoreType.DMA((3,)),
            pltpu.VMEM((8, 128), jnp.int32),
            pltpu.SMEM((8, 128), jnp.int32),
            pltpu.SemaphoreType.DMA,
        ],
        compiler_params=pltpu.CompilerParams(
            collective_id=0, has_side_effects=True, vmem_limit_bytes=56 * 1024 * 1024
        ),
    )(
        inner_cols,
        face_rows,
        face_counts,
        rhs.reshape(512, 128),
        inner_cols,
        send_blocks[None],
        contact_send[None],
        face_rows[None],
        contact_rows[None],
        contact_pair,
        inner_tiles,
        face_tiles,
        contact_tiles,
    )
    outs = pl.pallas_call(
        hand_over, out_shape=[out] * 3, in_specs=[vmem] * 3, out_specs=[vmem] * 3
    )(*outs)
    return tuple(x.reshape(64, 8, 128) for x in outs)


def solution(mesh):
    both = ("dom", "sub")
    field = P(None, None, both)
    devices = 1
    for axis in both:
        devices *= mesh.shape[axis]
    return jax.shard_map(
        functools.partial(shards, devices),
        mesh=mesh,
        in_specs=(
            field,
            P(None, None, None, both),
            P(None, both),
            P(both),
            P(both),
            P(both, None),
            field,
            P(both),
            P(both),
            P(both, None),
            field,
        ),
        out_specs=(field,) * 3,
        check_vma=False,
    )
```

```python
import functools

import jax
import jax.numpy as jnp
from jax import lax
from jax.experimental import pallas as pl
from jax.experimental.pallas import tpu as pltpu
from jax.sharding import PartitionSpec as P

F32 = jnp.float32
BF16 = jnp.bfloat16
APPS = 5
MESH = pl.DeviceIdType.MESH
PAD = 136
NT = (((1,), (1,)), ((), ()))


def stage_sizes(devices):
    bits = devices.bit_length() - 1
    first = min(3, bits - 2)
    second = min(3, bits - first - 1)
    return (1 << first, 1 << second, 1 << (bits - first - second))


def low_half(shape):
    return lax.broadcasted_iota(jnp.int32, shape, 1) < 64


def swap(x):
    return pltpu.roll(x, 64, 1)


def pair(x, y):
    low = low_half(x.shape)
    return jnp.where(low, x, swap(y)), jnp.where(low, swap(x), y)


def split(x):
    high = x.astype(BF16)
    return high, (x - high.astype(F32)).astype(BF16)


def split_wide(x):
    high = x.astype(BF16).astype(F32)
    return high, x - high


def dot(a, b):
    return jnp.dot(a, b, preferred_element_type=F32)


def dot_nt(a, b):
    return lax.dot_general(a, b, NT, preferred_element_type=F32)


def split_dot(product, a, b):
    rows = a.shape[0]
    out = product(jnp.concatenate(split(a), axis=0), b)
    return out[:rows] + out[rows:]


def block8(ref, index):
    return ref[pl.ds(pl.multiple_of(index * 8, 8), 8), :]


def put8(ref, index, value):
    ref[pl.ds(pl.multiple_of(index * 8, 8), 8), :] = value


def every8(first, count):
    return pl.ds(first, count, stride=8)


def kernel(
    devices,
    cols_s,
    frows_s,
    counts_s,
    rhs,
    cols_v,
    send_v,
    csend_v,
    frows_v,
    crows_v,
    pair_v,
    tiles_h,
    ftiles_h,
    ctiles_h,
    adjoint,
    residual,
    normal,
    tiles,
    ftiles,
    ctiles,
    wf0,
    wf1,
    w,
    ef,
    e,
    ohk,
    ohs,
    ohst,
    ohr,
    p01,
    p23,
    zs,
    z0,
    q,
    f0,
    fw,
    fs,
    u,
    xf,
    ps,
    uo,
    sbuf,
    rbuf,
    arsend,
    arrecv,
    xsend,
    xrecv,
    asend,
    arecv,
    fetched,
    crows_w,
    crows_s,
    crows_sem,
):
    fetches = [
        pltpu.make_async_copy(source, target, fetched.at[index])
        for index, (source, target) in enumerate(
            ((ftiles_h, ftiles), (ctiles_h, ctiles), (tiles_h, tiles))
        )
    ]
    for fetch in fetches:
        fetch.start()
    me = lax.axis_index("dom") * 2 + lax.axis_index("sub")
    sizes = stage_sizes(devices)

    def place(index):
        return (index // 2, lax.rem(index, 2))

    lower = lax.rem(me + devices - 1, devices)
    upper = lax.rem(me + 1, devices)
    partner = lax.rem(me + devices // 2, devices)

    def group_peers(stage):
        stride = 1
        for size in sizes[:stage]:
            stride *= size
        size = sizes[stage]
        mine = lax.rem(me // stride, size)
        return [me + (lax.rem(mine + i, size) - mine) * stride for i in range(1, size)]

    peers = [group_peers(stage) for stage in range(3)]
    ar_first = [sum(size - 1 for size in sizes[:stage]) for stage in range(3)]
    everyone = [lower, upper, partner] + peers[0] + peers[1] + peers[2]

    barrier = pltpu.get_barrier_semaphore()
    for other in everyone:
        pl.semaphore_signal(barrier, inc=1, device_id=place(other), device_id_type=MESH)

    row_id = lax.broadcasted_iota(jnp.int32, (128, 128), 0)
    for half in range(2):
        for k in range(4):
            at = half * 512 + k * 128
            ohk[:, at : at + 128] = jnp.where(cols_v[k : k + 1, :] == row_id, 1.0, 0.0).astype(BF16)
    picks = jnp.concatenate([send_v[...], csend_v[...]], axis=1) == row_id
    picks = jnp.where(picks, 1.0, 0.0)
    ohs[...] = jnp.concatenate([picks.astype(BF16)] * 2, axis=1)
    picks = picks.T.astype(BF16)
    ohst[...] = jnp.concatenate([picks] * 2, axis=1)
    lane_id = lax.broadcasted_iota(jnp.int32, (128, 128), 1)
    matches = jnp.broadcast_to(jnp.concatenate([pair_v[...]] * 2, axis=1), (128, 128)).T == lane_id
    rows = jnp.broadcast_to(jnp.concatenate([crows_v[...]] * 2, axis=1), (128, 128)).T
    rows = jnp.sum(jnp.where(matches & (row_id < 64), rows, 0), axis=0, keepdims=True)
    crows_w[...] = jnp.broadcast_to(rows, (8, 128))
    hand = pltpu.make_async_copy(crows_w, crows_s, crows_sem)
    hand.start()
    hand.wait()
    picks = jnp.concatenate([frows_v[...], rows[:, :64]], axis=1) == row_id
    picks = jnp.where(picks, 1.0, 0.0).astype(BF16)
    ohr[...] = jnp.concatenate([picks] * 2, axis=1)

    def prepare(a, carry):
        for half, out in ((0, wf0), (1, wf1)):
            x = tiles[2 * half : 2 * half + 2, a].reshape(128, 128)
            x = x.astype(F32).T
            out[pl.ds(a, 64, stride=PAD), :] = x[:64]
            out[pl.ds(64 + a, 64, stride=PAD), :] = x[64:]
        return carry

    def pack(i, carry):
        at = pl.ds(pl.multiple_of(i * 128, 128), 128)
        padded = pl.ds(pl.multiple_of(i * PAD, 8), 128)
        w[at, 0:128] = wf0[padded, :].astype(BF16)
        w[at, 128:256] = wf1[padded, :].astype(BF16)
        return carry

    def prepare_inner():
        fetches[2].wait()
        lax.fori_loop(0, 64, prepare, 0, unroll=8)
        lax.fori_loop(0, 64, pack, 0, unroll=4)

    for n in range(8):
        x = rhs[every8(n, 64), :]
        x = jnp.concatenate([x, x], axis=0).T
        u[:, n, :] = x
        f0[every8(n, 64), :] = jnp.where(low_half((64, 128)), x[:64], x[64:])

    slot = lax.broadcasted_iota(jnp.int32, (64, 64), 0)
    other_slot = lax.broadcasted_iota(jnp.int32, (64, 64), 1)
    side_a = (slot < 32) & (slot < counts_s[0, 0])
    side_b = (slot >= 32) & (slot - 32 < counts_s[0, 1])
    face_pick = jnp.where((slot == other_slot) & (side_a | side_b), 1.0, 0.0)
    contact_pick = jnp.where(pair_v[...] == slot, 1.0, 0.0)
    slot_picks = (face_pick.astype(BF16), contact_pick.astype(BF16))

    def prepare_slots(i, carry):
        for kind, source in enumerate((ftiles, ctiles)):
            parts = []
            for n in range(4):
                parts += [source[4 * i + n]] * 2
            x = dot_nt(slot_picks[kind], jnp.concatenate(parts, axis=0))
            for n in range(4):
                y = x[:, 128 * n : 128 * n + 128]
                for s2 in range(2):
                    at = 32 * s2
                    ef[pl.ds(kind * 16 * PAD + s2 * 64 + 4 * i + n, 16, stride=PAD), :] = jnp.where(
                        low_half((16, 128)), y[at : at + 16], y[at + 16 : at + 32]
                    )
        return carry

    for fetch in fetches[:2]:
        fetch.wait()
    lax.fori_loop(0, 16, prepare_slots, 0, unroll=4)

    def pack_slots(i, carry):
        at = pl.ds(pl.multiple_of(i * 128, 128), 128)
        e[at, :] = ef[pl.ds(pl.multiple_of(i * PAD, 8), 128), :].astype(BF16)
        return carry

    lax.fori_loop(0, 32, pack_slots, 0, unroll=8)

    def tile_at(ref, index):
        return ref[pl.ds(pl.multiple_of(index * 128, 128), 128), :]

    low8 = low_half((8, 128))
    zero8 = jnp.zeros((8, 128), F32)

    def spread(field):
        x = field[...]
        y = swap(x)
        low = low_half(x.shape)
        u[0:64] = jnp.where(low, x, y).reshape(64, 8, 128)
        u[64:128] = jnp.where(low, y, x).reshape(64, 8, 128)


    routes = ((lower, 0, 32, 32), (upper, 32, 64, 0), (partner, 64, 128, 64))

    def exchange(app, kind):
        copies = []
        for index in ((0, 1), (2,))[kind]:
            other, start, stop, to = routes[index]
            copy = pltpu.make_async_remote_copy(
                src_ref=sbuf.at[app, :, pl.ds(start, stop - start), :],
                dst_ref=rbuf.at[app, :, pl.ds(to, stop - start), :],
                send_sem=xsend.at[app, index],
                recv_sem=xrecv.at[app, index],
                device_id=place(other),
                device_id_type=MESH,
            )
            copy.start()
            copies.append(copy)
        return copies

    def reduce_start(which, step, value):
        stage = (1, 0, 2)[step]
        arsend[which, stage] = value
        for index, other in enumerate(peers[stage]):
            pltpu.make_async_remote_copy(
                src_ref=arsend.at[which, stage],
                dst_ref=arrecv.at[which, ar_first[stage] + index],
                send_sem=asend.at[which, stage],
                recv_sem=arecv.at[which, stage],
                device_id=place(other),
                device_id_type=MESH,
            ).start()

    def reduce_end(which, step):
        stage = (1, 0, 2)[step]
        arrived = arrecv.at[which, pl.ds(ar_first[stage], len(peers[stage]))]
        pltpu.make_async_copy(arrived, arrived, arecv.at[which, stage]).wait()
        pltpu.make_async_copy(arrived, arrived, asend.at[which, stage]).wait()
        total = arsend[which, stage]
        for index in range(len(peers[stage])):
            total = total + arrecv[which, ar_first[stage] + index]
        return total

    def transpose_slots(app):
        copies = []
        for kind, rows in enumerate((lambda i: frows_s[i], lambda i: crows_s[0, i])):

            def body(tp, carry):
                parts = []
                for h in range(2):
                    parts.append(jnp.where(low8, u[rows(16 * h + tp)], zero8))
                    parts.append(jnp.where(low8, zero8, u[rows(32 + 16 * h + tp)]))
                out = split_dot(dot, jnp.concatenate(parts, axis=0), tile_at(e, 16 * kind + tp))
                put8(ps, 32 * kind + tp, jnp.where(low8, out[0:8], out[16:24]))
                put8(ps, 32 * kind + 16 + tp, jnp.where(low8, out[8:16], out[24:32]))
                return carry

            lax.fori_loop(0, 16, body, 0, unroll=16)
            for np in range(4):
                at = 256 * kind + 2 * np
                x, y = pair(ps[every8(at, 32), :], ps[every8(at + 1, 32), :])
                sbuf[app, np, 64 * kind : 64 * kind + 64] = jnp.concatenate(
                    [x[:16], y[:16], x[16:], y[16:]], axis=0
                )
            if app == 0 and kind == 0:
                pl.semaphore_wait(barrier, len(everyone))
            copies += exchange(app, kind)
        return copies

    def transpose_inner(field):
        def body(jp, carry):
            high, rest = split_wide(block8(field, jp))
            parts = [
                jnp.where(low8, high, zero8),
                jnp.where(low8, rest, zero8),
                jnp.where(low8, zero8, high),
                jnp.where(low8, zero8, rest),
            ]
            out = dot(jnp.concatenate(parts, axis=0).astype(BF16), tile_at(w, jp))
            x = out[0:8] + out[8:16]
            y = out[16:24] + out[24:32]
            put8(p01, jp, x[:, :128])
            put8(p23, jp, x[:, 128:])
            put8(p01, 64 + jp, y[:, :128])
            put8(p23, 64 + jp, y[:, 128:])
            return carry

        lax.fori_loop(0, 64, body, 0, unroll=16)

    def put_turned(out, first, np, x):
        x = x.T
        out[every8(first + 2 * np, 64), :] = x[:64]
        out[every8(first + 2 * np + 1, 64), :] = x[64:]

    def halves(parts):
        x = jnp.concatenate(parts, axis=1)
        return jnp.concatenate(split(x), axis=0)

    def transpose_end(app, copies, result, send_app):
        parts = []
        for np in range(4):
            k0, k1 = pair(p01[every8(2 * np, 128), :], p01[every8(2 * np + 1, 128), :])
            k2, k3 = pair(p23[every8(2 * np, 128), :], p23[every8(2 * np + 1, 128), :])
            parts.append(jnp.concatenate([k0, k1, k2, k3], axis=0))
        zs[...] = dot(ohk[...], halves(parts))
        for copy in copies:
            copy.wait()
        low = low_half((128, 128))
        z = zs[...] + dot(ohs[...], halves([rbuf[app, np] for np in range(4)]))
        if send_app is not None:
            x = dot(ohst[...], jnp.concatenate(split(z), axis=0))
            for np in range(4):
                sbuf[send_app, np] = x[:, 128 * np : 128 * np + 128]
            copies = exchange(send_app, 0) + exchange(send_app, 1)
        for np in range(4):
            x = z[:, 128 * np : 128 * np + 128]
            if result is None:
                put_turned(p01, 0, np, x)
            else:
                other = swap(x)
                result[:, 2 * np, :] = jnp.where(low, x, other)
                result[:, 2 * np + 1, :] = jnp.where(low, other, x)
        return copies

    def forward_inner(field, result):
        def body(jp, carry):
            parts = []
            for j2 in range(2):
                j = j2 * 64 + jp
                v = [field[cols_s[k, j]] for k in range(4)]
                x = jnp.concatenate(
                    [jnp.where(low8, v[0], v[1]), jnp.where(low8, v[2], v[3])], axis=1
                )
                parts += list(split_wide(x))
            out = dot_nt(jnp.concatenate(parts, axis=0).astype(BF16), tile_at(w, jp))
            put8(result, jp, jnp.where(low8, out[0:8] + out[8:16], out[16:24] + out[24:32]))
            return carry

        lax.fori_loop(0, 64, body, 0, unroll=16)

    def forward_end(app, copies, result):
        low = low_half((64, 128))
        first = lax.rem(lax.broadcasted_iota(jnp.int32, (64, 128), 0) // 16, 2) == 0
        mine = low == first
        for kind in (1, 0):
            for copy in (copies[:2], copies[2:])[kind]:
                copy.wait()
            for np in range(4):
                x = rbuf[app, np, 64 * kind : 64 * kind + 64]
                y = swap(x)
                at = 512 * kind + 2 * np
                xf[every8(at, 64), :] = jnp.where(mine, jnp.where(first, x, y), 0.0)
                xf[every8(at + 1, 64), :] = jnp.where(mine, jnp.where(first, y, x), 0.0)

            def body(tp, carry):
                parts = []
                for h in range(2):
                    for s2 in range(2):
                        parts.append(block8(xf, 64 * kind + 32 * s2 + 16 * h + tp))
                tile = tile_at(e, 16 * kind + tp)
                out = split_dot(dot_nt, jnp.concatenate(parts, axis=0), tile)
                put8(uo, 32 * kind + tp, jnp.where(low8, out[0:8], out[8:16]))
                put8(uo, 32 * kind + 16 + tp, jnp.where(low8, out[16:24], out[24:32]))
                return carry

            lax.fori_loop(0, 16, body, 0, unroll=16)
        parts = []
        for np in range(4):
            s0, s1 = pair(uo[every8(2 * np, 64), :], uo[every8(2 * np + 1, 64), :])
            parts.append(jnp.concatenate([s0[:32], s1[:32], s0[32:], s1[32:]], axis=0))
        y = dot(ohr[...], halves(parts))
        sums = []
        for np in range(4):
            x = y[:, 128 * np : 128 * np + 128]
            for n, x in enumerate(pair(x[:64], x[64:])):
                sums.append(result[every8(2 * np + n, 64), :] + x)
        for n, x in enumerate(sums):
            result[every8(n, 64), :] = x

    def total(x):
        x = jnp.sum(x.reshape(-1, 8, 128), axis=0)
        return jnp.broadcast_to(jnp.sum(x, axis=1, keepdims=True), (8, 128))

    lane8 = lax.broadcasted_iota(jnp.int32, (8, 128), 1)

    def column(x, index):
        return jnp.broadcast_to(x[:, index : index + 1], (8, 128))

    def each(x, rows):
        return jnp.broadcast_to(x[None], (rows // 8, 8, 128)).reshape(rows, 128)

    copies = transpose_slots(0)
    prepare_inner()
    transpose_inner(f0)
    copies = transpose_end(0, copies, z0, 1)
    forward_inner(z0, fw)
    zz = total(z0[...] * z0[...]) * 0.5
    forward_end(1, copies, fw)
    ww = total(fw[...] * fw[...])
    reduce_start(0, 0, jnp.where(lane8 < 64, zz, ww))
    spread(fw)
    copies = transpose_slots(2)
    transpose_inner(fw)
    reduce_start(0, 1, reduce_end(0, 0))
    copies = transpose_end(2, copies, q, 3)
    forward_inner(q, fs)
    reduce_start(0, 2, reduce_end(0, 1))
    forward_end(3, copies, fs)
    sums = reduce_end(0, 2)
    zz0 = column(sums, 0)
    ww0 = column(sums, 64)
    alpha0 = zz0 / ww0
    s1 = fw[...] - each(alpha0, 512) * fs[...]
    fs[...] = s1
    z1 = z0[...] - alpha0[None] * q[...]
    zz = total(z1 * z1) * 0.5
    ss = total(s1 * s1)
    sw = total(s1 * fw[...])
    reduce_start(1, 0, jnp.where(lane8 < 32, zz, jnp.where(lane8 < 64, ss, sw)))
    spread(fs)
    copies = transpose_slots(4)
    transpose_inner(fs)
    reduce_start(1, 1, reduce_end(1, 0))
    transpose_end(4, copies, None, None)
    reduce_start(1, 2, reduce_end(1, 1))

    def gather_rows(field, np):
        top, bottom = pair(field[every8(2 * np, 64), :], field[every8(2 * np + 1, 64), :])
        return jnp.concatenate([top, bottom], axis=0)

    low = low_half((128, 128))
    for np in range(4):
        for source, out, first in ((z0, adjoint, 0), (q, p01, 512)):
            x = jnp.where(low, source[:, 2 * np, :], source[:, 2 * np + 1, :])
            put_turned(out, first, np, x)
        for source, out, first in ((f0, residual, 0), (fw, p23, 0), (fs, p23, 512)):
            put_turned(out, first, np, gather_rows(source, np))
    a0 = each(alpha0, 512)
    normal[...] = adjoint[...] - a0 * p01[512:1024]
    residual[...] = residual[...] - a0 * p23[0:512]

    sums = reduce_end(1, 2)
    zz1 = column(sums, 0)
    beta = zz1 / zz0
    ww1 = column(sums, 32) + beta * (2.0 * column(sums, 64) + beta * ww0)
    alpha1 = zz1 / ww1
    a1, b = each(alpha1, 512), each(beta, 512)
    x, z1 = adjoint[...], normal[...]
    adjoint[...] = a0 * x + a1 * (z1 + b * x)
    normal[...] = z1 - a1 * (p01[0:512] + b * p01[512:1024])
    residual[...] = residual[...] - a1 * (p23[512:1024] + b * p23[0:512])


def hand_over(*refs):
    for source, out in zip(refs[:3], refs[3:]):
        out[...] = source[...]


def shards(
    devices,
    rhs,
    inner_tiles,
    inner_cols,
    send_blocks,
    face_rows,
    face_counts,
    face_tiles,
    contact_send,
    contact_rows,
    contact_pair,
    contact_tiles,
):
    smem = pl.BlockSpec(memory_space=pltpu.SMEM)
    vmem = pl.BlockSpec(memory_space=pltpu.VMEM)
    copies = sum(size - 1 for size in stage_sizes(devices))
    out = jax.ShapeDtypeStruct((512, 128), F32)
    outs = pl.pallas_call(
        functools.partial(kernel, devices),
        out_shape=[out] * 3,
        in_specs=[smem] * 3 + [vmem] * 7 + [pl.BlockSpec(memory_space=pl.ANY)] * 3,
        out_specs=[vmem] * 3,
        scratch_shapes=[
            pltpu.VMEM(inner_tiles.shape, BF16),
            pltpu.VMEM(face_tiles.shape, BF16),
            pltpu.VMEM(contact_tiles.shape, BF16),
            pltpu.VMEM((64 * PAD, 128), F32),
            pltpu.VMEM((64 * PAD, 128), F32),
            pltpu.VMEM((8192, 256), BF16),
            pltpu.VMEM((32 * PAD, 128), F32),
            pltpu.VMEM((4096, 128), BF16),
            pltpu.VMEM((128, 1024), BF16),
            pltpu.VMEM((128, 256), BF16),
            pltpu.VMEM((128, 256), BF16),
            pltpu.VMEM((128, 256), BF16),
            pltpu.VMEM((1024, 128), F32),
            pltpu.VMEM((1024, 128), F32),
            pltpu.VMEM((128, 512), F32),
            pltpu.VMEM((128, 8, 128), F32),
            pltpu.VMEM((128, 8, 128), F32),
            pltpu.VMEM((512, 128), F32),
            pltpu.VMEM((512, 128), F32),
            pltpu.VMEM((512, 128), F32),
            pltpu.VMEM((128, 8, 128), F32),
            pltpu.VMEM((1024, 128), F32),
            pltpu.VMEM((512, 128), F32),
            pltpu.VMEM((512, 128), F32),
            pltpu.VMEM((APPS, 4, 128, 128), F32),
            pltpu.VMEM((APPS, 4, 128, 128), F32),
            pltpu.VMEM((2, 3, 8, 128), F32),
            pltpu.VMEM((2, copies, 8, 128), F32),
            pltpu.SemaphoreType.DMA((APPS, 3)),
            pltpu.SemaphoreType.DMA((APPS, 3)),
            pltpu.SemaphoreType.DMA((2, 3)),
            pltpu.SemaphoreType.DMA((2, 3)),
            pltpu.SemaphoreType.DMA((3,)),
            pltpu.VMEM((8, 128), jnp.int32),
            pltpu.SMEM((8, 128), jnp.int32),
            pltpu.SemaphoreType.DMA,
        ],
        compiler_params=pltpu.CompilerParams(
            collective_id=0, has_side_effects=True, vmem_limit_bytes=56 * 1024 * 1024
        ),
    )(
        inner_cols,
        face_rows,
        face_counts,
        rhs.reshape(512, 128),
        inner_cols,
        send_blocks[None],
        contact_send[None],
        face_rows[None],
        contact_rows[None],
        contact_pair,
        inner_tiles,
        face_tiles,
        contact_tiles,
    )
    outs = pl.pallas_call(
        hand_over, out_shape=[out] * 3, in_specs=[vmem] * 3, out_specs=[vmem] * 3
    )(*outs)
    return tuple(x.reshape(64, 8, 128) for x in outs)


def solution(mesh):
    both = ("dom", "sub")
    field = P(None, None, both)
    devices = 1
    for axis in both:
        devices *= mesh.shape[axis]
    return jax.shard_map(
        functools.partial(shards, devices),
        mesh=mesh,
        in_specs=(
            field,
            P(None, None, None, both),
            P(None, both),
            P(both),
            P(both),
            P(both, None),
            field,
            P(both),
            P(both),
            P(both, None),
            field,
        ),
        out_specs=(field,) * 3,
        check_vma=False,
    )
```
